32 devices in a mesh: items: 16 (over z, y, x), au: 2 (over core).
Axes of the slice: x: 2, y: 2, z: 4, core: 2. Of those that a mesh axis runs over, the one named last changes fastest.
Arguments:
- encoder_out: bfloat16 [64, 256, 512], P('items', 'au'), may hold values from -6 to 6
- labels: int32 [64, 64], P('items', 'au'), may hold values from 1 to 1023
- lengths: int32 [64], P('items'), may hold values from 55 to 63, as said below
- starts: int32 [64, 256], P('items', 'au'), may hold values from 0 to 59, as said below
- loss_cot: float32 [64], P('items'), may hold values from -6 to 6
- embed_table: bfloat16 [1024, 512], replicated, may hold values from -6 to 6
- conv_weight: bfloat16 [2, 128, 4, 4], replicated, may hold values from -2 to 2
- conv_bias: bfloat16 [512], replicated, may hold values from -3 to 3
- norm_gain: bfloat16 [512], replicated, may hold values from 0.5 to 1.5
- norm_bias: bfloat16 [512], replicated, may hold values from -2 to 2
- dec_weight: bfloat16 [512, 512], replicated, may hold values from -0.25 to 0.25
- dec_bias: bfloat16 [512], replicated, may hold values from -2 to 2
- enc_weight: bfloat16 [512, 512], replicated, may hold values from -0.25 to 0.25
- enc_bias: bfloat16 [512], replicated, may hold values from -2 to 2
- out_weight: bfloat16 [512, 1024], replicated, may hold values from -0.75 to 0.75
- out_bias: bfloat16 [1024], replicated, may hold values from -4 to 4
Outputs:
- losses: float32 [64], P(('items', 'au'))
- enc_grad: float32 [64, 256, 512], P('items', 'au')
- table_grad: float32 [1024, 512], replicated
- conv_weight_grad: float32 [2, 128, 4, 4], replicated
- conv_bias_grad: float32 [512], replicated
- gain_grad: float32 [512], replicated
- norm_bias_grad: float32 [512], replicated
- dec_weight_grad: float32 [512, 512], replicated
- dec_bias_grad: float32 [512], replicated
- enc_weight_grad: float32 [512, 512], replicated
- enc_bias_grad: float32 [512], replicated
- out_weight_grad: float32 [512, 1024], replicated
- out_bias_grad: float32 [1024], replicated
The draws below stay inside these ranges and needn't reach their ends.
Inputs may be any that keep to these rules, and one draw needn't show every extreme that they name: `labels`: entries at positions at or beyond an utterance's length are padding. `lengths`: the first utterance of every 4 has 63 labels. Never falling along the frames; frame 0 starts at 0; the last frame starts at the utterance's length - 4; consecutive frames differ by at most 3.
All inputs are finite; a program needn't handle non-finite values.
Results may differ from the reference program's by a relative error of at most 0.007.
Values may be sent and summed in bfloat16 or wider, within the bound.
A program may use at most 128 MiB of HBM per device.

```python
import jax
import jax.numpy as jnp
from jax import lax

UTT_DEV = 4
FRAMES = 256
POSITIONS = 64
WINDOW = 5
DEC = 512
ENC = 512
JOINT = 512
VOCAB = 1024
GROUPS = 128
UTTS = 64


def lengths_common(key):
    drawn = jax.random.randint(key, (UTTS,), POSITIONS - 9, POSITIONS, dtype=jnp.int32)
    leading = jnp.arange(UTTS, dtype=jnp.int32) % UTT_DEV == 0
    return jnp.where(leading, POSITIONS - 1, drawn)


def draw_lengths(key, part):
    return lengths_common(key)


def draw_starts(key, part):
    label_count = lengths_common(key)
    key = jax.random.fold_in(key, 11)
    jitter = jax.random.randint(key, (UTTS, FRAMES), -2, 1, dtype=jnp.int32)
    final_frame = jnp.arange(FRAMES, dtype=jnp.int32) == FRAMES - 1
    jitter = jnp.where(final_frame[None, :], 0, jitter)
    span_len = label_count + 1 - WINDOW
    baseline = jnp.arange(FRAMES, dtype=jnp.int32)[None, :] * span_len[:, None] // (FRAMES - 1)
    rising = lax.cummax(baseline + jitter, axis=1)
    return jnp.clip(rising, 0, span_len[:, None])


def plant(array, key, smallest, largest):
    place = [jax.random.randint(jax.random.fold_in(key, axis), (), 0, length) for axis, length in enumerate(array.shape)]
    main_axis = array.shape.index(max(array.shape))
    next_to = place[:main_axis] + [(place[main_axis] + 1) % array.shape[main_axis]] + place[main_axis + 1:]
    return array.at[tuple(place)].set(smallest).at[tuple(next_to)].set(largest)


def block_levels(rng, dims, split, least, high):
    level = 1.0
    for dim, parts in split:
        steps = jax.random.uniform(jax.random.fold_in(jax.random.fold_in(rng, 6), dim), (parts,), jnp.float32, least / len(split), high / len(split))
        level = level * jnp.repeat(jnp.exp(steps), dims[dim] // parts).reshape((-1,) + (1,) * (len(dims) - 1 - dim))
    return level


def normal_values(own_key, shape, width, bound, pieces=(), kind=jnp.bfloat16):
    factor_of = block_levels(own_key, shape, pieces, -0.22, 0.18) if pieces else 1.0
    values = jax.random.normal(own_key, shape, jnp.float32) * width * factor_of
    return jnp.minimum(jnp.maximum(values, -bound), bound).astype(kind)


def setup_inputs(seed: int = 0) -> dict:
    arg_keys = jax.random.split(jax.random.key(seed), 17)
    return {
        "encoder_out": normal_values(arg_keys[0], (UTTS, FRAMES, ENC), 1.0, 6.0, ((0, 16), (1, 2))),
        "labels": plant(jax.random.randint(arg_keys[1], (UTTS, POSITIONS), 1, VOCAB), jax.random.fold_in(arg_keys[1], 1), 1, VOCAB - 1).astype(jnp.int32),
        "lengths": draw_lengths(jax.random.fold_in(arg_keys[16], 71), 0),
        "starts": draw_starts(jax.random.fold_in(arg_keys[16], 71), 0),
        "loss_cot": normal_values(arg_keys[4], (UTTS,), 1.0, 6.0, ((0, 16),), jnp.float32),
        "embed_table": normal_values(arg_keys[5], (VOCAB, DEC), 1.0, 6.0),
        "conv_weight": normal_values(arg_keys[6], (2, GROUPS, 4, 4), 8 ** -0.5, 2.0),
        "conv_bias": normal_values(arg_keys[7], (DEC,), 0.5, 3.0),
        "norm_gain": jnp.clip(1.0 + 0.1 * jax.random.normal(arg_keys[8], (DEC,), jnp.float32), 0.5, 1.5).astype(jnp.bfloat16),
        "norm_bias": normal_values(arg_keys[9], (DEC,), 0.3, 2.0),
        "dec_weight": normal_values(arg_keys[10], (DEC, JOINT), DEC ** -0.5, 0.25),
        "dec_bias": normal_values(arg_keys[11], (JOINT,), 0.3, 2.0),
        "enc_weight": normal_values(arg_keys[12], (ENC, JOINT), ENC ** -0.5, 0.25),
        "enc_bias": normal_values(arg_keys[13], (JOINT,), 0.3, 2.0),
        "out_weight": normal_values(arg_keys[14], (JOINT, VOCAB), (JOINT // 8) ** -0.5, 0.75),
        "out_bias": normal_values(arg_keys[15], (VOCAB,), 1.0, 4.0),
    }


NEGATIVE_FILL = -1e+30
NORM_EPS = 1e-05

@jax.custom_vjp
def low(v):
    return lax.optimization_barrier(v.astype(jnp.bfloat16)).astype(jnp.float32)

@jax.custom_vjp
def low_back(v):
    return v

def low_keep(v):
    return (low(v), None)

def low_pass(kept, grad):
    return (grad,)

def back_keep(v):
    return (v, None)

def back_low(kept, grad):
    return (low(grad),)
low.defvjp(low_keep, low_pass)
low_back.defvjp(back_keep, back_low)

def grouped(values, kernel):
    shaped = values.reshape(values.shape[0], kernel.shape[0], kernel.shape[1])
    mixed = jnp.einsum('pgi,gio->pgo', shaped, kernel, precision=lax.Precision.HIGHEST)
    return mixed.reshape(values.shape[0], -1)

def norm_tail(conv_out, gain_values, shift_values):
    row_mean = lax.optimization_barrier(jnp.mean(conv_out, axis=-1, keepdims=True))
    centered = conv_out - row_mean
    row_var = lax.optimization_barrier(jnp.mean(centered * centered, axis=-1, keepdims=True))
    normed = centered * lax.rsqrt(row_var + NORM_EPS)
    return jax.nn.silu(normed * gain_values + shift_values)

def emit_row(entry_vec, emit_now):
    columns = [entry_vec[0]]
    for column in range(1, entry_vec.shape[0]):
        columns.append(jnp.logaddexp(entry_vec[column], columns[-1] + emit_now[column - 1]))
    return jnp.stack(columns)

def utterance_loss(weights, frames_in, tokens, length, begins):
    table, kernel, kernel_bias, gain_values, shift_values, dec_w, dec_b, enc_w, enc_b, out_w, out_b = weights
    prev_ids = jnp.concatenate([jnp.zeros((1,), jnp.int32), tokens[:-1].astype(jnp.int32)])
    embedded = jnp.take(table, prev_ids, axis=0)
    before = jnp.concatenate([jnp.zeros((1, embedded.shape[1]), embedded.dtype), embedded[:-1]], axis=0)
    conv_out = grouped(before, kernel[0]) + grouped(embedded, kernel[1]) + kernel_bias
    hidden = norm_tail(conv_out, gain_values, shift_values)
    dec_proj = low_back(low(jnp.dot(low(hidden), dec_w, precision=lax.Precision.HIGHEST) + dec_b))
    enc_proj = low_back(low(jnp.dot(frames_in, enc_w, precision=lax.Precision.HIGHEST) + enc_b))
    offsets = jnp.arange(WINDOW, dtype=jnp.int32)
    upos = begins[:, None].astype(jnp.int32) + offsets[None, :]
    picked = jnp.take(dec_proj, upos, axis=0)
    joint_low = low(jnp.tanh(enc_proj[:, None, :] + picked))
    logits = low_back(jnp.einsum('tsj,jv->tsv', joint_low, out_w, precision=lax.Precision.HIGHEST) + out_b)
    log_norm = jax.nn.logsumexp(logits, axis=-1)
    blank_lp = logits[:, :, 0] - log_norm
    targets = jnp.take(tokens, upos, axis=0).astype(jnp.int32)
    emit_raw = jnp.take_along_axis(logits, targets[:, :, None], axis=2)[:, :, 0] - log_norm
    emit_lp = jnp.where(upos < length, emit_raw, NEGATIVE_FILL)
    entry_first = jnp.where(offsets == 0, 0.0, NEGATIVE_FILL).astype(blank_lp.dtype)
    alpha_first = emit_row(entry_first, emit_lp[0])
    moves = (begins[1:] - begins[:-1]).astype(jnp.int32)

    def advance_step(alpha_prev, inputs):
        blank_prev, emit_now, moved = inputs
        padded = jnp.concatenate([alpha_prev + blank_prev, jnp.full((WINDOW,), NEGATIVE_FILL, blank_prev.dtype)])
        entry_vec = jnp.take(padded, moved + offsets)
        return (emit_row(entry_vec, emit_now), None)
    alpha_last, _ = lax.scan(advance_step, alpha_first, (blank_lp[:-1], emit_lp[1:], moves))
    log_total = alpha_last[WINDOW - 1] + blank_lp[-1, WINDOW - 1]
    return -log_total / FRAMES

def reference(encoder_out, labels, lengths, starts, loss_cot, embed_table, conv_weight, conv_bias, norm_gain, norm_bias, dec_weight, dec_bias, enc_weight, enc_bias, out_weight, out_bias):
    weights = tuple((item.astype(jnp.float32) for item in (embed_table, conv_weight, conv_bias, norm_gain, norm_bias, dec_weight, dec_bias, enc_weight, enc_bias, out_weight, out_bias)))
    frames_all = encoder_out.astype(jnp.float32)

    def objective(weight_set, frame_set):
        single = jax.checkpoint(lambda packed: utterance_loss(weight_set, packed[0], packed[1], packed[2], packed[3]))
        losses = lax.map(single, (frame_set, labels, lengths, starts))
        return (jnp.sum(losses * loss_cot), losses)
    objective_val, pullback, losses = jax.vjp(objective, weights, frames_all, has_aux=True)
    weight_grads, frame_grad = pullback(jnp.ones_like(objective_val))
    return (losses, frame_grad, weight_grads[0], weight_grads[1], weight_grads[2], weight_grads[3], weight_grads[4], weight_grads[5], weight_grads[6], weight_grads[7], weight_grads[8], weight_grads[9], weight_grads[10])
```

```python
import functools

import jax
import jax.numpy as jnp
from jax import lax
from jax.experimental import pallas as pl
from jax.experimental.pallas import tpu as pltpu
from jax.sharding import PartitionSpec as P

WINDOW = 5
NEGATIVE_FILL = -1e30
NORM_EPS = 1e-05
F32 = jnp.float32
BF16 = jnp.bfloat16
MIB = 1 << 20
MESH = pl.DeviceIdType.MESH


def dot(a, b):
    return lax.dot_general(a, b, (((1,), (0,)), ((), ())), preferred_element_type=F32)


def dot_nt(a, b):
    return lax.dot_general(a, b, (((1,), (1,)), ((), ())), preferred_element_type=F32)


def halves(x):
    high = x.astype(BF16)
    return high, (x - high.astype(F32)).astype(BF16)


def iota(shape, dim):
    return lax.broadcasted_iota(jnp.int32, shape, dim)


def column_of(row):
    return jnp.transpose(jnp.broadcast_to(row, (128, row.shape[1])))


def shift_rows(x, moved):
    out = x
    for step in (1, 2, 3):
        out = jnp.where(moved == step, pltpu.roll(x, step, 0), out)
    return out


def lattice(blank, emit, moved, scale, frames):
    lanes = blank.shape[1]
    row = iota((8, lanes), 0)
    lane = iota((8, lanes), 1) % frames
    window_row = row < WINDOW
    before = jnp.where(
        lane == 0, jnp.where(row == 0, 0.0, NEGATIVE_FILL), pltpu.roll(blank, 1, 1)
    )
    path = jnp.where(row == 0, 0.0, NEGATIVE_FILL)
    prefix = []
    for k in range(WINDOW):
        if k:
            path = jnp.where(
                row == k, 0.0, jnp.where(row < k, path + emit[k - 1 : k], NEGATIVE_FILL)
            )
        prefix.append(shift_rows(path, moved) + before)
    reach = 1
    while reach < frames:
        earlier = [pltpu.roll(column, reach, 1) for column in prefix]
        joined = []
        for k in range(WINDOW):
            terms = [earlier[i] + prefix[k][i : i + 1] for i in range(WINDOW)]
            top = functools.reduce(jnp.maximum, terms)
            total = functools.reduce(jnp.add, [jnp.exp(term - top) for term in terms])
            joined.append(top + jnp.log(total))
        prefix = [jnp.where(lane >= reach, new, old) for new, old in zip(joined, prefix)]
        reach *= 2
    alpha = jnp.concatenate(
        [column[:1] for column in prefix] + [jnp.full((8 - WINDOW, lanes), NEGATIVE_FILL, F32)], axis=0
    )
    leaving = alpha + blank
    arrived = pltpu.roll(leaving, 1, 1)
    entry = arrived
    for step in (1, 2, 3):
        entry = jnp.where(moved == step, pltpu.roll(arrived, 8 - step, 0), entry)
    entry = jnp.where(lane == 0, jnp.where(row == 0, 0.0, NEGATIVE_FILL), entry)
    lead = pltpu.roll(alpha + emit, 1, 0) - entry
    from_emit = jnp.where(window_row & (row > 0), 1.0 / (1.0 + jnp.exp(-lead)), 0.0)
    from_entry = jnp.where(row == 0, 1.0, jnp.where(window_row, 1.0 / (1.0 + jnp.exp(lead)), 0.0))
    suffix = []
    flow = jnp.zeros((8, lanes), F32)
    for n in range(WINDOW):
        flow = jnp.where(row == n, from_entry, flow * from_emit[n : n + 1])
        suffix.append(jnp.where(window_row, shift_rows(flow, moved), 0.0))
    reach = 1
    while reach < frames:
        later = [pltpu.roll(column, lanes - reach, 1) for column in suffix]
        joined = []
        for n in range(WINDOW):
            terms = [suffix[i] * later[n][i : i + 1] for i in range(WINDOW)]
            joined.append(functools.reduce(jnp.add, terms))
        suffix = [
            jnp.where(lane < frames - reach, new, old) for new, old in zip(joined, suffix)
        ]
        reach *= 2
    outward = jnp.where(
        lane == frames - 1,
        jnp.where(row == WINDOW - 1, 1.0, 0.0),
        pltpu.roll(suffix[WINDOW - 1], lanes - 1, 1),
    )
    state = jnp.zeros((1, lanes), F32)
    upward = [None] * WINDOW
    for k in range(WINDOW - 1, -1, -1):
        upward[k] = state
        state = outward[k : k + 1] + state
        if k:
            state = state * from_emit[k : k + 1]
    emitted = jnp.concatenate(upward + [jnp.zeros((8 - WINDOW, lanes), F32)], axis=0)
    return leaving, outward * scale, emitted * scale


BLOCKS = 6
UNITS = BLOCKS // 2
LEVELS = 32000.0

WHOLE = 12582912.0


def coded(value):
    top = jnp.maximum(jnp.max(jnp.abs(value), axis=0, keepdims=True), 1e-30)
    code = (value * (LEVELS / top) + WHOLE) - WHOLE
    return code.astype(jnp.int32).astype(jnp.int16), top * (1.0 / LEVELS)


def decoded(code, scale):
    return code.astype(jnp.int32).astype(F32) * scale


def wide(row, count):
    return jnp.concatenate([row] * count, axis=1)


def main_kernel(
    share,
    rounds,
    lengths_ref,
    cot_ref,
    labels_own_ref,
    starts_own_ref,
    conv_w_ref,
    conv_b_ref,
    gain_ref,
    shift_ref,
    dec_b_ref,
    enc_b_ref,
    out_b_ref,
    enc_hbm,
    table_hbm,
    dec_w_hbm,
    enc_w_hbm,
    out_w_hbm,
    loss_ref,
    enc_g_own_hbm,
    enc_g_far_hbm,
    small_total_ref,
    total_hbm,
    labels_far_ref,
    starts_far_ref,
    enc_own_ref,
    enc_far_ref,
    table_ref,
    dec_w_ref,
    enc_w_ref,
    out_w_ref,
    out_wt_ref,
    bias_ref,
    dec_t_ref,
    enc_t_ref,
    raw_a_ref,
    raw_b_ref,
    exp_ref,
    act_ref,
    low_ref,
    glow_ref,
    blank_ref,
    emit_ref,
    inv_ref,
    wide_label_ref,
    blank_g_ref,
    emit_g_ref,
    factor_ref,
    enc_sum_ref,
    dec_sum_ref,
    starts_ref,
    grads_ref,
    small_ref,
    enc_g_send_ref,
    enc_g_own_ref,
    total_ref,
    send_core,
    send_one,
    send_two,
    take_core,
    take_one,
    take_two,
    send_line,
    take_line,
    send_scale,
    take_scale,
    small_now,
    small_take,
    far_now,
    far_take,
    load_sems,
    swap_sems,
    code_sems,
    scale_sems,
    gather_sems,
    sent_sems,
    small_sems,
    far_sems,
    enc_sems,
    out_sems,
):
    core = lax.axis_index("au")
    item = lax.axis_index("items")
    utts = share
    half = starts_own_ref.shape[1]
    positions = 2 * labels_own_ref.shape[1]
    frames = 2 * half
    width, vocab = out_w_ref.shape
    rows = utts * positions
    lanes = utts * frames
    chunks = utts * WINDOW
    first = core * share

    loads = []
    for at, (source, target) in enumerate(
        (
            (enc_w_hbm, enc_w_ref),
            (enc_hbm.at[pl.ds(first, share)], enc_own_ref),
            (out_w_hbm, out_w_ref),
            (table_hbm, table_ref),
            (dec_w_hbm, dec_w_ref),
        )
    ):
        loads.append(pltpu.make_async_copy(source, target, load_sems.at[at]))
        loads[-1].start()
    load_enc_w, load_enc, load_out_w, load_table, load_dec_w = loads

    bit_x = item % 2
    bit_y = (item // 2) % 2
    line = (item // 4) % 4
    base = item - line * 4
    other = {"items": item, "au": 1 - core}
    to_x = {"items": item + 1 - 2 * bit_x, "au": core}
    to_y = {"items": item + 2 - 4 * bit_y, "au": core}
    peers = []
    for step in (1, 2, 3):
        low = line % 2
        high = line // 2
        low = 1 - low if step % 2 else low
        high = 1 - high if step // 2 else high
        peers.append((low + 2 * high, {"items": base + 4 * (low + 2 * high), "au": core}))
    far = []
    for r in range(rounds):
        bit = (item // (16 << r)) % 2
        far.append({"items": item + (16 << r) * (1 - 2 * bit), "au": core})
    everyone = [other, to_x, to_y] + [peer for _, peer in peers] + far

    barrier = pltpu.get_barrier_semaphore()
    for device in everyone:
        pl.semaphore_signal(barrier, inc=1, device_id=device, device_id_type=MESH)
    pl.semaphore_wait(barrier, len(everyone))

    pending = []

    def send(source, target, sems, device):
        copy = pltpu.make_async_remote_copy(
            src_ref=source,
            dst_ref=target,
            send_sem=sems.at[0],
            recv_sem=sems.at[1],
            device_id=device,
            device_id_type=MESH,
        )
        copy.start()
        pending.append(copy)
        return copy

    def push(source, target, sent, landed, device):
        pltpu.make_async_remote_copy(
            src_ref=source,
            dst_ref=target,
            send_sem=sent,
            recv_sem=landed,
            device_id=device,
            device_id_type=MESH,
        ).start()

    def settled(ref, sem):
        pltpu.make_async_copy(ref, ref, sem).wait()

    swap_labels = send(labels_own_ref, labels_far_ref, swap_sems.at[0], other)
    swap_starts = send(starts_own_ref, starts_far_ref, swap_sems.at[1], other)
    swap_enc = send(
        enc_hbm.at[pl.ds((1 - core) * share, share)], enc_far_ref, swap_sems.at[2], other
    )

    flights = {}
    depth = grads_ref.shape[4]
    piece = depth // 4

    def on_line(place):
        return pl.ds(pl.multiple_of(place * piece, piece), piece)

    def pack(value, code_ref, scale_ref):
        value = value.reshape(-1, width)
        code, scale = coded(value)
        code_ref[...] = code.reshape(code_ref.shape)
        scale_ref[...] = scale

    def unpack(code_ref, scale_ref):
        return decoded(code_ref[...], scale_ref[...])

    def ship(u, slot, source, target, scale_at, device):
        push(source, target, sent_sems.at[u, 0], code_sems.at[u, slot], device)
        push(
            send_scale.at[(u,) + scale_at],
            take_scale.at[(u,) + scale_at],
            sent_sems.at[u, 1],
            scale_sems.at[u, slot],
            device,
        )

    def landed(u, slot, target, scale_at):
        settled(target, code_sems.at[u, slot])
        settled(take_scale.at[(u,) + scale_at], scale_sems.at[u, slot])

    def held(j, u):
        return grads_ref.at[2 * u + j, core]

    def stage0(u):
        for j in range(2):
            pack(grads_ref[2 * u + j, 1 - core], send_core.at[u, j], send_scale.at[u, 0, j])
        ship(u, 0, send_core.at[u], take_core.at[u], (0,), other)

    def stage1(u):
        ways = (
            (0, (1 - bit_x,), (bit_x,), to_x),
            (1, (slice(None), 1 - bit_y), (slice(None), bit_y), to_y),
        )
        landed(u, 0, take_core.at[u], (0,))

        def part(j, at):
            return held(j, u)[at] + decoded(take_core[(u, j) + at], take_scale[u, 0, j])

        for j, away, _, _ in ways:
            pack(part(j, away), send_one.at[u, j], send_scale.at[u, 1, j])
        for j, _, _, device in ways:
            ship(u, 1 + j, send_one.at[u, j], take_one.at[u, j], (1, j), device)
        for j, _, keep, _ in ways:
            held(j, u)[keep] = part(j, keep)

    def stage2(u):
        ways = (
            (0, (bit_x, 1 - bit_y), bit_y, to_y),
            (1, (1 - bit_x, bit_y), bit_x, to_x),
        )
        for j in range(2):
            landed(u, 1 + j, take_one.at[u, j], (1, j))
        for j, away, here, _ in ways:
            value = decoded(take_one[u, j, 1 - here], take_scale[u, 1, j])
            pack(held(j, u)[away] + value, send_two.at[u, j], send_scale.at[u, 2, j])
        for j, _, _, device in ways:
            ship(u, 3 + j, send_two.at[u, j], take_two.at[u, j], (2, j), device)
        for j, _, here, _ in ways:
            held(j, u)[bit_x, bit_y] += decoded(take_one[u, j, here], take_scale[u, 1, j])

    def stage3(u):
        for j in range(2):
            landed(u, 3 + j, take_two.at[u, j], (2, j))
        for j in range(2):
            value = held(j, u)[bit_x, bit_y] + unpack(take_two.at[u, j], take_scale.at[u, 2, j])
            pack(value, send_line.at[u, j], send_scale.at[u, 3, j])
            held(j, u)[bit_x, bit_y] = value
        for step, (place, device) in enumerate(peers):
            push(
                send_line.at[u, :, on_line(place), :],
                take_line.at[u, step],
                sent_sems.at[u, 0],
                code_sems.at[u, 5],
                device,
            )
            push(
                send_scale.at[u, 3],
                take_scale.at[u, 3 + step],
                sent_sems.at[u, 1],
                scale_sems.at[u, 5],
                device,
            )

    def stage4(u):
        landed(u, 5, take_line.at[u], (pl.ds(3, 3),))
        for j in range(2):
            value = held(j, u)[bit_x, bit_y, on_line(line), :]
            for step in range(3):
                value = value + unpack(take_line.at[u, step, j], take_scale.at[u, 3 + step, j])
            for r in range(rounds):
                far_now[r, 2 * u + j] = value
                send(
                    far_now.at[r, 2 * u + j],
                    far_take.at[r, 2 * u + j],
                    far_sems.at[r, 2 * u + j],
                    far[r],
                ).wait_recv()
                value = value + far_take[r, 2 * u + j]
            total_ref[2 * u + j, core, bit_x, bit_y, on_line(line), :] = value.astype(BF16)
        place = total_ref.at[pl.ds(2 * u, 2), core, bit_x, bit_y, on_line(line), :]
        for _, device in peers:
            push(place, place, sent_sems.at[u, 2], gather_sems.at[u, 0], device)

    def spread_on(u, slot, place, device):
        push(place, place, sent_sems.at[u, 2], gather_sems.at[u, slot], device)

    def stage5(u):
        three = total_ref.at[pl.ds(2 * u, 2), core, bit_x, bit_y, pl.ds(0, 3 * piece), :]
        settled(three, gather_sems.at[u, 0])
        for j, device in ((0, to_y), (1, to_x)):
            spread_on(u, 1 + j, total_ref.at[2 * u + j, core, bit_x, bit_y], device)

    def stage6(u):
        for j, at, device in ((0, (bit_x,), to_x), (1, (slice(None), bit_y), to_y)):
            settled(total_ref.at[2 * u + j, core, bit_x, bit_y], gather_sems.at[u, 1 + j])
            spread_on(u, 3 + j, total_ref.at[(2 * u + j, core) + at], device)

    def stage7(u):
        for j in range(2):
            settled(total_ref.at[2 * u + j, core, bit_x], gather_sems.at[u, 3 + j])
        spread_on(u, 5, total_ref.at[pl.ds(2 * u, 2), core], other)

    outs = []

    def leave(source, target, at):
        outs.append(pltpu.make_async_copy(source, target, out_sems.at[at]))
        outs[-1].start()

    def stage8(u):
        settled(total_ref.at[pl.ds(2 * u, 2), core], gather_sems.at[u, 5])
        leave(total_ref.at[pl.ds(2 * u, 2)], total_hbm.at[pl.ds(2 * u, 2)], u)

    def all_sent(u):
        rows_sent = 2 * (4 + 2 + 1) * depth + 6 * piece
        by_lanes = glow_ref.at[pl.ds(0, rows_sent // 2), pl.ds(0, 2 * width)]
        settled(by_lanes, sent_sems.at[u, 0])
        settled(by_lanes, sent_sems.at[u, 2])
        settled(enc_t_ref.at[pl.ds(0, 24), pl.ds(0, width // 2)], sent_sems.at[u, 1])

    part_rows = small_ref.shape[0] // 2

    def small_send(slot, source, device):
        flights["s", slot] = send(source, small_take.at[slot], small_sems.at[slot], device)

    def small_step(stage):
        mine = pl.ds(pl.multiple_of(core * part_rows, part_rows), part_rows)
        if stage == 0:
            theirs = pl.ds(pl.multiple_of((1 - core) * part_rows, part_rows), part_rows)
            small_send(0, small_ref.at[theirs, :], other)
        elif stage == 1:
            flights["s", 0].wait_recv()
            small_now[0] = small_ref[mine, :] + small_take[0]
            small_send(1, small_now.at[0], to_x)
        elif stage == 2:
            flights["s", 1].wait_recv()
            small_now[1] = small_now[0] + small_take[1]
            small_send(2, small_now.at[1], to_y)
        elif stage == 3:
            flights["s", 2].wait_recv()
            small_now[2] = small_now[1] + small_take[2]
            for step, (_, device) in enumerate(peers):
                small_send(3 + step, small_now.at[2], device)
        elif stage == 4:
            for step in range(3):
                flights["s", 3 + step].wait_recv()
            value = (small_now[2] + small_take[3]) + (small_take[4] + small_take[5])
            for r in range(rounds):
                small_now[3 + r] = value
                small_send(6 + r, small_now.at[3 + r], far[r])
                flights["s", 6 + r].wait_recv()
                value = value + small_take[6 + r]
            small_total_ref[mine, :] = value
            place = small_total_ref.at[mine, :]
            flights["s", "last"] = send(place, place, small_sems.at[6 + rounds], other)
        elif stage == 5:
            flights["s", "last"].wait_recv()

    def own_lanes(b):
        return pl.ds(pl.multiple_of(b * frames + core * half, half), half)

    def far_lanes(b):
        return pl.ds(pl.multiple_of(b * frames + (1 - core) * half, half), half)

    def project(source, place):
        value = source[...].reshape(utts * half, enc_w_ref.shape[0])
        enc_proj = dot(value, enc_w_ref[...]) + enc_b_ref[...].astype(F32)[None, :]
        turned = jnp.transpose(enc_proj.astype(BF16).astype(F32))
        for b in range(utts):
            enc_t_ref[:, place(b)] = turned[:, b * half : (b + 1) * half]

    load_enc_w.wait()
    load_enc.wait()
    project(enc_own_ref, own_lanes)
    load_out_w.wait()
    out_wt_ref[pl.ds(0, vocab), :] = jnp.transpose(out_w_ref[...])
    bias_ref[pl.ds(0, vocab), :] = column_of(out_b_ref[...].astype(F32)[None, :])
    small_ref[...] = jnp.zeros(small_ref.shape, F32)
    blank_ref[...] = jnp.full(blank_ref.shape, NEGATIVE_FILL, F32)
    emit_ref[...] = jnp.full(emit_ref.shape, NEGATIVE_FILL, F32)
    low_ref[pl.ds(width, 16), :] = jnp.ones((16, low_ref.shape[1]), BF16)
    spread = jnp.where(iota((width, 4), 0) % 4 == iota((width, 4), 1), 1.0, 0.0).astype(BF16)
    same_group = iota((width, width), 0) // 4 == iota((width, width), 1) // 4
    group = width // 4
    widen = jnp.where(iota((group, width), 0) == iota((group, width), 1) // 4, 1.0, 0.0).astype(BF16)
    lane_out = iota((1, width), 1) % 4
    taps = []
    for tap in range(2):
        kernel_rows = []
        for i in range(4):
            spans = dot(conv_w_ref[tap, i], widen)
            row = jnp.zeros((1, width), F32)
            for o in range(4):
                row = jnp.where(lane_out == o, spans[o : o + 1], row)
            kernel_rows.append(row)
        kernel_rows = jnp.concatenate(kernel_rows, axis=0).astype(BF16)
        taps.append(jnp.where(same_group, dot(spread, kernel_rows), 0.0).astype(BF16))

    swap_labels.wait_recv()
    swap_starts.wait_recv()
    pieces = []
    for b in range(utts):
        own = labels_own_ref[pl.ds(first + b, 1), :].astype(F32)
        theirs = labels_far_ref[pl.ds(first + b, 1), :].astype(F32)
        pieces += [jnp.where(core == 0, own, theirs), jnp.where(core == 0, theirs, own)]
    label_row = jnp.concatenate(pieces, axis=1)
    for b in range(utts):
        for place, source in ((core, starts_own_ref), (1 - core, starts_far_ref)):
            starts_ref[pl.ds(b, 1), pl.ds(pl.multiple_of(place * half, half), half)] = source[
                pl.ds(first + b, 1), :
            ]
    within = iota((1, rows), 1) % positions
    token_row = jnp.where(within == 0, 0.0, pltpu.roll(label_row, 1, 1))
    label_col = column_of(label_row)
    token_col = column_of(token_row)
    vocab_lane = iota((rows, 128), 1).astype(F32)

    def one_hot(column):
        parts = [
            jnp.where(vocab_lane + float(at) == column, 1.0, 0.0).astype(BF16)
            for at in range(0, vocab, 128)
        ]
        return jnp.concatenate(parts, axis=1)

    row_within = iota((rows, width), 0) % positions
    load_table.wait()
    emb = dot(one_hot(token_col), table_ref[...])
    emb_prev = jnp.where(row_within == 0, 0.0, pltpu.roll(emb, 1, 0))
    emb_low = emb.astype(BF16)
    prev_low = emb_prev.astype(BF16)
    conv_out = dot(prev_low, taps[0]) + dot(emb_low, taps[1])
    conv_out = conv_out + conv_b_ref[...].astype(F32)[None, :]
    mean = jnp.mean(conv_out, axis=1, keepdims=True)
    centered = conv_out - mean
    rstd = lax.rsqrt(jnp.mean(centered * centered, axis=1, keepdims=True) + NORM_EPS)
    normed = centered * rstd
    gain = gain_ref[...].astype(F32)[None, :]
    scaled = normed * gain + shift_ref[...].astype(F32)[None, :]
    sigmoid = 1.0 / (1.0 + jnp.exp(-scaled))
    hidden = scaled * sigmoid
    hidden_low = hidden.astype(BF16)
    load_dec_w.wait()
    dec_proj = dot(hidden_low, dec_w_ref[...]) + dec_b_ref[...].astype(F32)[None, :]
    dec_t_ref[...] = jnp.transpose(dec_proj).astype(BF16)

    label_hot = one_hot(label_col)
    picks = pl.ds(vocab, rows)
    out_wt_ref[picks, :] = dot(label_hot, out_wt_ref[pl.ds(0, vocab), :]).astype(BF16)
    bias_ref[picks, :] = dot(label_hot, bias_ref[pl.ds(0, vocab), :].astype(BF16))
    wide_label = wide(label_col, frames // 128)
    swap_enc.wait_recv()
    project(enc_far_ref, far_lanes)

    block = 256

    def selector(b, k):
        begin = starts_ref[pl.ds(b, 1), :] + (k + b * positions)
        return iota((rows, frames), 0) == begin

    def chunk_lanes(c):
        return pl.ds(pl.multiple_of(c * frames, frames), frames)

    def utt_lanes(c):
        return pl.ds(pl.multiple_of((c // WINDOW) * frames, frames), frames)

    def activate(c):
        hot = jnp.where(selector(c // WINDOW, c % WINDOW), 1.0, 0.0).astype(BF16)
        act = jnp.tanh(enc_t_ref[:, utt_lanes(c)] + dot(dec_t_ref[...], hot))
        act_ref[c] = act
        low_ref[pl.ds(0, width), chunk_lanes(c)] = act.astype(BF16)

    def score(c, raw_ref):
        low = low_ref[pl.ds(0, width), chunk_lanes(c)]
        raw_ref[...] = dot(out_wt_ref[...], low) + wide(bias_ref[...], frames // 128)

    def normalise(c, raw_ref):
        b = c // WINDOW
        k = c % WINDOW
        top = jnp.max(raw_ref[pl.ds(0, vocab), :], axis=0, keepdims=True)
        total = jnp.zeros((1, frames), F32)
        for v in range(0, vocab, block):
            part = jnp.exp(raw_ref[pl.ds(v, block), :] - top)
            exp_ref[c, pl.ds(v, block), :] = part
            total = total + jnp.sum(part, axis=0, keepdims=True)
        log_norm = top + jnp.log(total)
        picked = selector(b, k)
        target = jnp.where(picked, raw_ref[pl.ds(vocab, rows), :], 0.0)
        target = jnp.sum(target, axis=0, keepdims=True) - log_norm
        live = starts_ref[pl.ds(b, 1), :] + k < lengths_ref[first + b]
        here = (pl.ds(k, 1), utt_lanes(c))
        blank_ref[here] = raw_ref[pl.ds(0, 1), :] - log_norm
        emit_ref[here] = jnp.where(live, target, NEGATIVE_FILL)
        inv_ref[here] = 1.0 / total
        wide_label_ref[here] = jnp.sum(jnp.where(picked, wide_label, 0.0), axis=0, keepdims=True)

    activate(0)
    activate(1)
    score(0, raw_a_ref)

    def forward(i, carry):
        c = 2 * i
        score(c + 1, raw_b_ref)
        normalise(c, raw_a_ref)
        activate(jnp.minimum(c + 2, chunks - 1))
        score(jnp.minimum(c + 2, chunks - 1), raw_a_ref)
        normalise(c + 1, raw_b_ref)
        activate(jnp.minimum(c + 3, chunks - 1))
        return carry

    lax.fori_loop(0, chunks // 2, forward, 0)

    starts_row = jnp.concatenate([starts_ref[b : b + 1, :] for b in range(utts)], axis=1)
    lane_row = iota((1, lanes), 1)
    moved = jnp.where(lane_row % frames == 0, 0, starts_row - pltpu.roll(starts_row, 1, 1))
    scale = jnp.zeros((1, lanes), F32)
    for b in range(utts):
        scale = jnp.where(lane_row // frames == b, -cot_ref[first + b] / frames, scale)
    leaving, blank_g, emit_g = lattice(blank_ref[...], emit_ref[...], moved, scale, frames)
    blank_g_ref[...] = blank_g
    emit_g_ref[...] = emit_g
    factor_ref[...] = -(blank_g + emit_g) * inv_ref[...]
    ends = iota((8, lanes), 1)
    for b in range(utts):
        last = (ends == (b + 1) * frames - 1) & (iota((8, lanes), 0) == WINDOW - 1)
        loss_ref[b] = -jnp.sum(jnp.where(last, leaving, 0.0)) / frames

    def logits_back(v):
        ids = iota((block, frames), 0) + v
        for c in range(chunks):
            b, k = c // WINDOW, c % WINDOW
            here = (slice(k, k + 1), slice(b * frames, (b + 1) * frames))
            blank_now, emit_now, factor = blank_g_ref[here], emit_g_ref[here], factor_ref[here]
            label_now = wide_label_ref[here].astype(jnp.int32)
            other_part = jnp.where(ids == 0, blank_now, 0.0) if v == 0 else 0.0
            grad = exp_ref[c, pl.ds(v, block), :] * factor + jnp.where(
                ids == label_now, emit_now, other_part
            )
            glow_ref[pl.ds(v, block), pl.ds(c * frames, frames)] = grad.astype(BF16)

    def weight_back(v):
        total = dot_nt(low_ref[...], glow_ref[pl.ds(v, block), :])
        grads_ref[v // width, :, :, :, :, pl.ds(v % width, block)] = total[:width].reshape(
            grads_ref.shape[1:5] + (block,)
        )
        small_ref[pl.ds(13 + v // width, 1), pl.ds(v % width, block)] = total[width : width + 1]

    logits_back(0)
    for v in range(0, vocab, block):
        weight_back(v)
        if v + block < vocab:
            logits_back(v + block)

    stage0(0)

    enc_sum_ref[...] = jnp.zeros(enc_sum_ref.shape, F32)
    dec_sum_ref[...] = jnp.zeros(dec_sum_ref.shape, F32)

    def pull(c, back_ref):
        back_ref[pl.ds(0, width), :] = dot(out_w_ref[...], glow_ref[:, chunk_lanes(c)])

    def settle(c, back_ref):
        act = act_ref[c]
        grad = back_ref[pl.ds(0, width), :] * (1.0 - act * act)
        enc_sum_ref[:, utt_lanes(c)] += grad
        hot = jnp.where(selector(c // WINDOW, c % WINDOW), 1.0, 0.0).astype(BF16)
        both = dot_nt(jnp.concatenate(halves(grad), axis=0), hot)
        dec_sum_ref[...] += both[:width] + both[width:]

    def backward(i, carry):
        c = 2 * i
        pull(c + 1, raw_b_ref)
        settle(c, raw_a_ref)
        pull(jnp.minimum(c + 2, chunks - 1), raw_a_ref)
        settle(c + 1, raw_b_ref)
        return carry

    pull(0, raw_a_ref)
    lax.fori_loop(0, 2, backward, 0)
    stage1(0)
    lax.fori_loop(2, chunks // 2, backward, 0)
    stage2(0)

    enc_b_grad = jnp.zeros((1, width), F32)
    enc_w_grad = jnp.zeros((enc_w_ref.shape[0], width), F32)
    for source, place, target in (
        (enc_far_ref, far_lanes, enc_g_send_ref),
        (enc_own_ref, own_lanes, enc_g_own_ref),
    ):
        enc_g = jnp.concatenate([enc_sum_ref[:, place(b)] for b in range(utts)], axis=1)
        enc_g = jnp.transpose(enc_g).astype(BF16)
        target[...] = enc_g.reshape(utts, half, width)
        value = source[...].reshape(utts * half, enc_w_ref.shape[0])
        enc_w_grad = enc_w_grad + dot(jnp.transpose(value), enc_g)
        enc_b_grad = enc_b_grad + jnp.sum(enc_g.astype(F32), axis=0, keepdims=True)
    grads_ref[2] = enc_w_grad.reshape(grads_ref.shape[1:])
    enc_copy = send(enc_g_send_ref, enc_g_far_hbm, enc_sems, other)
    leave(enc_g_own_ref, enc_g_own_hbm, UNITS)
    stage3(0)

    dec_g = jnp.transpose(dec_sum_ref[...]).astype(BF16)
    dec_b_grad = jnp.sum(dec_g.astype(F32), axis=0, keepdims=True)
    grads_ref[3] = dot(jnp.transpose(hidden).astype(BF16), dec_g).reshape(grads_ref.shape[1:])
    stage0(1)
    hidden_grad = dot_nt(dec_g, dec_w_ref[...])
    scaled_grad = hidden_grad * (sigmoid * (1.0 + scaled * (1.0 - sigmoid)))
    gain_grad = jnp.sum(scaled_grad * normed, axis=0, keepdims=True)
    shift_grad = jnp.sum(scaled_grad, axis=0, keepdims=True)
    normed_grad = scaled_grad * gain
    conv_grad = rstd * (
        normed_grad
        - jnp.mean(normed_grad, axis=1, keepdims=True)
        - normed * jnp.mean(normed_grad * normed, axis=1, keepdims=True)
    )
    high, rest = halves(conv_grad)
    prev_grad = dot_nt(high, taps[0]) + dot_nt(rest, taps[0])
    emb_grad = dot_nt(high, taps[1]) + dot_nt(rest, taps[1])
    emb_grad = emb_grad + jnp.where(
        row_within == positions - 1, 0.0, pltpu.roll(prev_grad, rows - 1, 0)
    )
    high, rest = halves(emb_grad)
    token_hot_t = jnp.where(
        iota((vocab, rows), 0) == token_row.astype(jnp.int32), 1.0, 0.0
    ).astype(BF16)
    for part in range(vocab // width):
        hot = token_hot_t[part * width : (part + 1) * width]
        table_grad = dot(hot, high) + dot(hot, rest)
        grads_ref[4 + part] = table_grad.reshape(grads_ref.shape[1:])
    stage0(2)
    stage1(1)
    stage4(0)

    conv_b_grad = jnp.sum(conv_grad, axis=0, keepdims=True)
    turned = halves(jnp.transpose(conv_grad))
    fold = jnp.where(iota((8, width), 1) % 4 == iota((8, width), 0), 1.0, 0.0).astype(BF16)
    for tap, source in enumerate((prev_low, emb_low)):
        outer = jnp.where(same_group, dot(turned[0], source) + dot(turned[1], source), 0.0)
        high, rest = halves(outer)
        folded = dot(fold, high) + dot(fold, rest)
        small_ref[pl.ds(4 * tap, 4), :] = folded[:4]
    for at, value in enumerate((conv_b_grad, gain_grad, shift_grad, dec_b_grad, enc_b_grad)):
        small_ref[pl.ds(8 + at, 1), :] = value

    small_step(0)
    stage1(2)
    stage2(1)
    stage5(0)
    small_step(1)
    stage2(2)
    stage3(1)
    stage6(0)
    small_step(2)
    stage3(2)
    stage4(1)
    stage7(0)
    small_step(3)
    stage4(2)
    stage5(1)
    stage8(0)
    small_step(4)
    stage5(2)
    stage6(1)
    small_step(5)
    stage6(2)
    stage7(1)
    stage7(2)
    stage8(1)
    stage8(2)
    for u in range(UNITS):
        all_sent(u)
    enc_copy.wait_recv()
    for copy in pending:
        copy.wait_send()
    for copy in outs:
        copy.wait()


def finish_kernel(
    share,
    loss_in_ref,
    small_ref,
    total_hbm,
    enc_g_own_hbm,
    enc_g_far_hbm,
    enc_w_hbm,
    loss_ref,
    enc_grad_hbm,
    table_hbm,
    conv_w_ref,
    conv_b_ref,
    gain_ref,
    shift_ref,
    dec_w_hbm,
    dec_b_ref,
    enc_w_grad_hbm,
    enc_b_ref,
    out_w_hbm,
    out_b_ref,
    enc_grad_ref,
    table_ref,
    dec_w_ref,
    enc_w_grad_ref,
    out_w_ref,
    total_ref,
    enc_g_own_ref,
    enc_g_far_ref,
    enc_w_ref,
    load_sems,
    sems,
):
    core = lax.axis_index("au")
    width = enc_w_ref.shape[1]
    loads = []
    for i in range(BLOCKS):
        loads.append((total_hbm.at[i], total_ref.at[i]))
    loads += [
        (enc_w_hbm, enc_w_ref),
        (enc_g_own_hbm, enc_g_own_ref),
        (enc_g_far_hbm, enc_g_far_ref),
    ]
    loads = [
        pltpu.make_async_copy(source, target, load_sems.at[at])
        for at, (source, target) in enumerate(loads)
    ]
    for load in loads:
        load.start()
    copies = []

    def leave(source, target):
        copies.append(pltpu.make_async_copy(source, target, sems.at[len(copies)]))
        copies[-1].start()

    for b in range(share):
        loss_ref[b] = loss_in_ref[b]
    for at, target in enumerate((conv_b_ref, gain_ref, shift_ref, dec_b_ref, enc_b_ref)):
        target[...] = small_ref[8 + at, :]
    out_b_ref[:width] = small_ref[13, :]
    out_b_ref[width:] = small_ref[14, :]
    group = width // 4
    high, rest = halves(small_ref[:8, :])
    last = (small_ref[:8, :] - high.astype(F32) - rest.astype(F32)).astype(BF16)
    for i in range(4):
        take = iota((width, group), 0) == 4 * iota((width, group), 1) + i
        take = jnp.where(take, 1.0, 0.0).astype(BF16)
        picked = dot(high, take) + dot(rest, take) + dot(last, take)
        for tap in range(2):
            conv_w_ref[tap, i] = picked[4 * tap : 4 * tap + 4]

    every = pl.ds(0, width)
    for i, target, home, where in (
        (0, out_w_ref, out_w_hbm, (every, pl.ds(0, width))),
        (1, out_w_ref, out_w_hbm, (every, pl.ds(width, width))),
        (2, enc_w_grad_ref, enc_w_grad_hbm, (every, every)),
        (3, dec_w_ref, dec_w_hbm, (every, every)),
        (4, table_ref, table_hbm, (pl.ds(0, width), every)),
        (5, table_ref, table_hbm, (pl.ds(width, width), every)),
    ):
        loads[i].wait()
        target[where] = total_ref[i].astype(F32).reshape(width, width)
        leave(target.at[where], home.at[where])
    loads[BLOCKS].wait()
    for at, source, place in (
        (BLOCKS + 1, enc_g_own_ref, core),
        (BLOCKS + 2, enc_g_far_ref, 1 - core),
    ):
        loads[at].wait()
        utts, half, _ = source.shape
        grad = dot_nt(source[...].reshape(utts * half, width), enc_w_ref[...])
        mine = pl.ds(place * share, share)
        enc_grad_ref[mine] = grad.reshape(utts, half, enc_w_ref.shape[0])
        leave(enc_grad_ref.at[mine], enc_grad_hbm.at[mine])
    for copy in copies:
        copy.wait()


def on_device(
    item_count,
    encoder_out,
    labels,
    lengths,
    starts,
    loss_cot,
    embed_table,
    conv_weight,
    conv_bias,
    norm_gain,
    norm_bias,
    dec_weight,
    dec_bias,
    enc_weight,
    enc_bias,
    out_weight,
    out_bias,
):
    utt_count, half, enc_dim = encoder_out.shape
    dec_dim = embed_table.shape[1]
    width, vocab = out_weight.shape
    share = utt_count // 2
    frames = 2 * half
    pairs = share * frames * WINDOW
    rows = share * 2 * labels.shape[1]
    lanes = share * frames
    chunks = share * WINDOW
    rounds = (item_count // 16).bit_length() - 1
    split = (2, 2, 2, width // 8, width)
    deep = max(rounds, 1)
    vmem = pl.BlockSpec(memory_space=pltpu.VMEM)
    smem = pl.BlockSpec(memory_space=pltpu.SMEM)
    anywhere = pl.BlockSpec(memory_space=pl.ANY)
    struct = jax.ShapeDtypeStruct
    mem = pltpu.VMEM
    dma = pltpu.SemaphoreType.DMA
    code = jnp.int16

    losses, enc_g_own, enc_g_far, small, totals = pl.pallas_call(
        functools.partial(main_kernel, share, rounds),
        out_shape=(
            struct((share,), F32),
            struct((share, half, width), BF16),
            struct((share, half, width), BF16),
            struct((16, width), F32),
            struct((BLOCKS,) + split, BF16),
        ),
        in_specs=[smem] * 2 + [vmem] * 9 + [anywhere] * 5,
        out_specs=(smem, anywhere, anywhere, vmem, anywhere),
        scratch_shapes=[
            mem(labels.shape, labels.dtype),
            mem(starts.shape, starts.dtype),
            mem((share, half, enc_dim), BF16),
            mem((share, half, enc_dim), BF16),
            mem(embed_table.shape, BF16),
            mem(dec_weight.shape, BF16),
            mem(enc_weight.shape, BF16),
            mem(out_weight.shape, BF16),
            mem((vocab + rows, width), BF16),
            mem((vocab + rows, 128), F32),
            mem((width, rows), BF16),
            mem((width, lanes), F32),
            mem((vocab + rows, frames), F32),
            mem((vocab + rows, frames), F32),
            mem((chunks, vocab, frames), F32),
            mem((chunks, width, frames), F32),
            mem((width + 16, pairs), BF16),
            mem((vocab, pairs), BF16),
        ]
        + [mem((8, lanes), F32)] * 7
        + [
            mem((width, lanes), F32),
            mem((width, rows), F32),
            mem((8, frames), jnp.int32),
            mem((BLOCKS,) + split, F32),
            mem((16, width), F32),
            mem((share, half, width), BF16),
            mem((share, half, width), BF16),
            mem((BLOCKS,) + split, BF16),
        ]
        + [
            mem((UNITS, 2) + split[1:], code),
            mem((UNITS, 2) + split[2:], code),
            mem((UNITS, 2) + split[3:], code),
        ]
        * 2
        + [
            mem((UNITS, 2, split[3], width), code),
            mem((UNITS, 3, 2, split[3] // 4, width), code),
            mem((UNITS, 6, 2, 1, width), F32),
            mem((UNITS, 6, 2, 1, width), F32),
            mem((3 + rounds, 8, width), F32),
            mem((6 + rounds, 8, width), F32),
            mem((deep, BLOCKS, split[3] // 4, width), F32),
            mem((deep, BLOCKS, split[3] // 4, width), F32),
            dma((5,)),
            dma((3, 2)),
            dma((UNITS, 6)),
            dma((UNITS, 6)),
            dma((UNITS, 6)),
            dma((UNITS, 3)),
            dma((7 + rounds, 2)),
            dma((deep, BLOCKS, 2)),
            dma((2,)),
            dma((UNITS + 1,)),
        ],
        compiler_params=pltpu.CompilerParams(
            collective_id=0, has_side_effects=True, vmem_limit_bytes=58 * MIB
        ),
        name="main",
    )(
        lengths,
        loss_cot,
        labels,
        starts,
        jnp.transpose(conv_weight, (0, 2, 3, 1)),
        conv_bias,
        norm_gain,
        norm_bias,
        dec_bias,
        enc_bias,
        out_bias,
        encoder_out,
        embed_table,
        dec_weight,
        enc_weight,
        out_weight,
    )

    vector = struct((width,), F32)
    square = struct((width, width), F32)
    outs = pl.pallas_call(
        functools.partial(finish_kernel, share),
        out_shape=(
            struct((share,), F32),
            struct(encoder_out.shape, F32),
            struct(embed_table.shape, F32),
            struct((2, 4, 4, dec_dim // 4), F32),
            vector,
            vector,
            vector,
            square,
            vector,
            square,
            vector,
            struct(out_weight.shape, F32),
            struct(out_bias.shape, F32),
        ),
        in_specs=[smem, vmem] + [anywhere] * 4,
        out_specs=(smem, anywhere, anywhere) + (vmem,) * 4 + (anywhere, vmem) * 3,
        scratch_shapes=[
            mem(encoder_out.shape, F32),
            mem(embed_table.shape, F32),
            mem((width, width), F32),
            mem((width, width), F32),
            mem(out_weight.shape, F32),
            mem((BLOCKS,) + split, BF16),
            mem((share, half, width), BF16),
            mem((share, half, width), BF16),
            mem(enc_weight.shape, BF16),
            dma((BLOCKS + 3,)),
            dma((BLOCKS + 2,)),
        ],
        compiler_params=pltpu.CompilerParams(vmem_limit_bytes=62 * MIB),
        name="finish",
    )(losses, small, totals, enc_g_own, enc_g_far, enc_weight)
    return outs[:3] + (jnp.transpose(outs[3], (0, 3, 1, 2)),) + outs[4:]


def solution(mesh):
    in_specs = (
        P("items", "au", None),
        P("items", "au"),
        P("items"),
        P("items", "au"),
        P("items"),
    ) + (P(),) * 11
    out_specs = (P(("items", "au")), P("items", "au", None)) + (P(),) * 11
    return jax.shard_map(
        functools.partial(on_device, mesh.shape["items"]),
        mesh=mesh,
        in_specs=in_specs,
        out_specs=out_specs,
        check_vma=False,
    )
```

```python
import functools

import jax
import jax.numpy as jnp
from jax import lax
from jax.experimental import pallas as pl
from jax.experimental.pallas import tpu as pltpu
from jax.sharding import PartitionSpec as P

WINDOW = 5
NEGATIVE_FILL = -1e30
NORM_EPS = 1e-05
F32 = jnp.float32
BF16 = jnp.bfloat16
MIB = 1 << 20
MESH = pl.DeviceIdType.MESH


def dot(a, b):
    return lax.dot_general(a, b, (((1,), (0,)), ((), ())), preferred_element_type=F32)


def dot_nt(a, b):
    return lax.dot_general(a, b, (((1,), (1,)), ((), ())), preferred_element_type=F32)


def halves(x):
    high = x.astype(BF16)
    return high, (x - high.astype(F32)).astype(BF16)


def iota(shape, dim):
    return lax.broadcasted_iota(jnp.int32, shape, dim)


def column_of(row):
    return jnp.transpose(jnp.broadcast_to(row, (128, row.shape[1])))


def shift_rows(x, moved):
    out = x
    for step in (1, 2, 3):
        out = jnp.where(moved == step, pltpu.roll(x, step, 0), out)
    return out


def lattice(blank, emit, moved, scale, frames):
    lanes = blank.shape[1]
    row = iota((8, lanes), 0)
    lane = iota((8, lanes), 1) % frames
    window_row = row < WINDOW
    before = jnp.where(
        lane == 0, jnp.where(row == 0, 0.0, NEGATIVE_FILL), pltpu.roll(blank, 1, 1)
    )
    path = jnp.where(row == 0, 0.0, NEGATIVE_FILL)
    prefix = []
    for k in range(WINDOW):
        if k:
            path = jnp.where(
                row == k, 0.0, jnp.where(row < k, path + emit[k - 1 : k], NEGATIVE_FILL)
            )
        prefix.append(shift_rows(path, moved) + before)
    reach = 1
    while reach < frames:
        earlier = [pltpu.roll(column, reach, 1) for column in prefix]
        joined = []
        for k in range(WINDOW):
            terms = [earlier[i] + prefix[k][i : i + 1] for i in range(WINDOW)]
            top = functools.reduce(jnp.maximum, terms)
            total = functools.reduce(jnp.add, [jnp.exp(term - top) for term in terms])
            joined.append(top + jnp.log(total))
        prefix = [jnp.where(lane >= reach, new, old) for new, old in zip(joined, prefix)]
        reach *= 2
    alpha = jnp.concatenate(
        [column[:1] for column in prefix] + [jnp.full((8 - WINDOW, lanes), NEGATIVE_FILL, F32)], axis=0
    )
    leaving = alpha + blank
    arrived = pltpu.roll(leaving, 1, 1)
    entry = arrived
    for step in (1, 2, 3):
        entry = jnp.where(moved == step, pltpu.roll(arrived, 8 - step, 0), entry)
    entry = jnp.where(lane == 0, jnp.where(row == 0, 0.0, NEGATIVE_FILL), entry)
    lead = pltpu.roll(alpha + emit, 1, 0) - entry
    from_emit = jnp.where(window_row & (row > 0), 1.0 / (1.0 + jnp.exp(-lead)), 0.0)
    from_entry = jnp.where(row == 0, 1.0, jnp.where(window_row, 1.0 / (1.0 + jnp.exp(lead)), 0.0))
    suffix = []
    flow = jnp.zeros((8, lanes), F32)
    for n in range(WINDOW):
        flow = jnp.where(row == n, from_entry, flow * from_emit[n : n + 1])
        suffix.append(jnp.where(window_row, shift_rows(flow, moved), 0.0))
    reach = 1
    while reach < frames:
        later = [pltpu.roll(column, lanes - reach, 1) for column in suffix]
        joined = []
        for n in range(WINDOW):
            terms = [suffix[i] * later[n][i : i + 1] for i in range(WINDOW)]
            joined.append(functools.reduce(jnp.add, terms))
        suffix = [
            jnp.where(lane < frames - reach, new, old) for new, old in zip(joined, suffix)
        ]
        reach *= 2
    outward = jnp.where(
        lane == frames - 1,
        jnp.where(row == WINDOW - 1, 1.0, 0.0),
        pltpu.roll(suffix[WINDOW - 1], lanes - 1, 1),
    )
    state = jnp.zeros((1, lanes), F32)
    upward = [None] * WINDOW
    for k in range(WINDOW - 1, -1, -1):
        upward[k] = state
        state = outward[k : k + 1] + state
        if k:
            state = state * from_emit[k : k + 1]
    emitted = jnp.concatenate(upward + [jnp.zeros((8 - WINDOW, lanes), F32)], axis=0)
    return leaving, outward * scale, emitted * scale


BLOCKS = 6
UNITS = BLOCKS // 2
LEVELS = 32000.0

WHOLE = 12582912.0


def coded(value):
    top = jnp.maximum(jnp.max(jnp.abs(value), axis=0, keepdims=True), 1e-30)
    code = (value * (LEVELS / top) + WHOLE) - WHOLE
    return code.astype(jnp.int32).astype(jnp.int16), top * (1.0 / LEVELS)


def decoded(code, scale):
    return code.astype(jnp.int32).astype(F32) * scale


def wide(row, count):
    return jnp.concatenate([row] * count, axis=1)


def main_kernel(
    share,
    rounds,
    lengths_ref,
    cot_ref,
    labels_own_ref,
    starts_own_ref,
    conv_w_ref,
    conv_b_ref,
    gain_ref,
    shift_ref,
    dec_b_ref,
    enc_b_ref,
    out_b_ref,
    enc_hbm,
    table_hbm,
    dec_w_hbm,
    enc_w_hbm,
    out_w_hbm,
    loss_ref,
    enc_g_own_hbm,
    enc_g_far_hbm,
    small_total_hbm,
    total_hbm,
    labels_far_ref,
    starts_far_ref,
    enc_own_ref,
    enc_far_ref,
    table_ref,
    dec_w_ref,
    enc_w_ref,
    out_w_ref,
    out_wt_ref,
    bias_ref,
    dec_t_ref,
    enc_t_ref,
    raw_a_ref,
    raw_b_ref,
    exp_ref,
    act_ref,
    low_ref,
    glow_ref,
    blank_ref,
    emit_ref,
    inv_ref,
    wide_label_ref,
    blank_g_ref,
    emit_g_ref,
    factor_ref,
    enc_sum_ref,
    dec_sum_ref,
    starts_ref,
    grads_ref,
    small_ref,
    enc_g_send_ref,
    enc_g_own_ref,
    total_ref,
    small_total_ref,
    send_core,
    send_one,
    send_two,
    take_core,
    take_one,
    take_two,
    send_line,
    take_line,
    send_scale,
    take_scale,
    small_now,
    small_take,
    far_now,
    far_take,
    load_sems,
    swap_sems,
    code_sems,
    scale_sems,
    gather_sems,
    sent_sems,
    small_sems,
    far_sems,
    enc_sems,
    out_sems,
):
    core = lax.axis_index("au")
    item = lax.axis_index("items")
    utts = share
    half = starts_own_ref.shape[1]
    positions = 2 * labels_own_ref.shape[1]
    frames = 2 * half
    width, vocab = out_w_ref.shape
    rows = utts * positions
    lanes = utts * frames
    chunks = utts * WINDOW
    first = core * share

    loads = []
    for at, (source, target) in enumerate(
        (
            (enc_w_hbm, enc_w_ref),
            (enc_hbm.at[pl.ds(first, share)], enc_own_ref),
            (out_w_hbm, out_w_ref),
            (table_hbm, table_ref),
            (dec_w_hbm, dec_w_ref),
        )
    ):
        loads.append(pltpu.make_async_copy(source, target, load_sems.at[at]))
        loads[-1].start()
    load_enc_w, load_enc, load_out_w, load_table, load_dec_w = loads

    bit_x = item % 2
    bit_y = (item // 2) % 2
    line = (item // 4) % 4
    base = item - line * 4
    other = {"items": item, "au": 1 - core}
    to_x = {"items": item + 1 - 2 * bit_x, "au": core}
    to_y = {"items": item + 2 - 4 * bit_y, "au": core}
    peers = []
    for step in (1, 2, 3):
        low = line % 2
        high = line // 2
        low = 1 - low if step % 2 else low
        high = 1 - high if step // 2 else high
        peers.append((low + 2 * high, {"items": base + 4 * (low + 2 * high), "au": core}))
    far = []
    for r in range(rounds):
        bit = (item // (16 << r)) % 2
        far.append({"items": item + (16 << r) * (1 - 2 * bit), "au": core})
    everyone = [other, to_x, to_y] + [peer for _, peer in peers] + far

    barrier = pltpu.get_barrier_semaphore()
    for device in everyone:
        pl.semaphore_signal(barrier, inc=1, device_id=device, device_id_type=MESH)
    pl.semaphore_wait(barrier, len(everyone))

    pending = []

    def send(source, target, sems, device):
        copy = pltpu.make_async_remote_copy(
            src_ref=source,
            dst_ref=target,
            send_sem=sems.at[0],
            recv_sem=sems.at[1],
            device_id=device,
            device_id_type=MESH,
        )
        copy.start()
        pending.append(copy)
        return copy

    def push(source, target, sent, landed, device):
        pltpu.make_async_remote_copy(
            src_ref=source,
            dst_ref=target,
            send_sem=sent,
            recv_sem=landed,
            device_id=device,
            device_id_type=MESH,
        ).start()

    def settled(ref, sem):
        pltpu.make_async_copy(ref, ref, sem).wait()

    swap_labels = send(labels_own_ref, labels_far_ref, swap_sems.at[0], other)
    swap_starts = send(starts_own_ref, starts_far_ref, swap_sems.at[1], other)
    swap_enc = send(
        enc_hbm.at[pl.ds((1 - core) * share, share)], enc_far_ref, swap_sems.at[2], other
    )

    flights = {}
    depth = grads_ref.shape[4]
    piece = depth // 4

    def on_line(place):
        return pl.ds(pl.multiple_of(place * piece, piece), piece)

    def pack(value, code_ref, scale_ref):
        value = value.reshape(-1, width)
        code, scale = coded(value)
        code_ref[...] = code.reshape(code_ref.shape)
        scale_ref[...] = scale

    def unpack(code_ref, scale_ref):
        return decoded(code_ref[...], scale_ref[...])

    def ship(u, slot, source, target, scale_at, device):
        push(source, target, sent_sems.at[u, 0], code_sems.at[u, slot], device)
        push(
            send_scale.at[(u,) + scale_at],
            take_scale.at[(u,) + scale_at],
            sent_sems.at[u, 1],
            scale_sems.at[u, slot],
            device,
        )

    def landed(u, slot, target, scale_at):
        settled(target, code_sems.at[u, slot])
        settled(take_scale.at[(u,) + scale_at], scale_sems.at[u, slot])

    def held(j, u):
        return grads_ref.at[2 * u + j, core]

    def stage0(u):
        for j in range(2):
            pack(grads_ref[2 * u + j, 1 - core], send_core.at[u, j], send_scale.at[u, 0, j])
        ship(u, 0, send_core.at[u], take_core.at[u], (0,), other)

    def stage1(u):
        ways = (
            (0, (1 - bit_x,), (bit_x,), to_x),
            (1, (slice(None), 1 - bit_y), (slice(None), bit_y), to_y),
        )
        landed(u, 0, take_core.at[u], (0,))

        def part(j, at):
            return held(j, u)[at] + decoded(take_core[(u, j) + at], take_scale[u, 0, j])

        for j, away, _, _ in ways:
            pack(part(j, away), send_one.at[u, j], send_scale.at[u, 1, j])
        for j, _, _, device in ways:
            ship(u, 1 + j, send_one.at[u, j], take_one.at[u, j], (1, j), device)
        for j, _, keep, _ in ways:
            held(j, u)[keep] = part(j, keep)

    def stage2(u):
        ways = (
            (0, (bit_x, 1 - bit_y), bit_y, to_y),
            (1, (1 - bit_x, bit_y), bit_x, to_x),
        )
        for j in range(2):
            landed(u, 1 + j, take_one.at[u, j], (1, j))
        for j, away, here, _ in ways:
            value = decoded(take_one[u, j, 1 - here], take_scale[u, 1, j])
            pack(held(j, u)[away] + value, send_two.at[u, j], send_scale.at[u, 2, j])
        for j, _, _, device in ways:
            ship(u, 3 + j, send_two.at[u, j], take_two.at[u, j], (2, j), device)
        for j, _, here, _ in ways:
            held(j, u)[bit_x, bit_y] += decoded(take_one[u, j, here], take_scale[u, 1, j])

    def stage3(u):
        for j in range(2):
            landed(u, 3 + j, take_two.at[u, j], (2, j))
        for j in range(2):
            value = held(j, u)[bit_x, bit_y] + unpack(take_two.at[u, j], take_scale.at[u, 2, j])
            pack(value, send_line.at[u, j], send_scale.at[u, 3, j])
            held(j, u)[bit_x, bit_y] = value
        for step, (place, device) in enumerate(peers):
            push(
                send_line.at[u, :, on_line(place), :],
                take_line.at[u, step],
                sent_sems.at[u, 0],
                code_sems.at[u, 5],
                device,
            )
            push(
                send_scale.at[u, 3],
                take_scale.at[u, 3 + step],
                sent_sems.at[u, 1],
                scale_sems.at[u, 5],
                device,
            )

    def stage4(u):
        landed(u, 5, take_line.at[u], (pl.ds(3, 3),))
        for j in range(2):
            value = held(j, u)[bit_x, bit_y, on_line(line), :]
            for step in range(3):
                value = value + unpack(take_line.at[u, step, j], take_scale.at[u, 3 + step, j])
            for r in range(rounds):
                far_now[r, 2 * u + j] = value
                send(
                    far_now.at[r, 2 * u + j],
                    far_take.at[r, 2 * u + j],
                    far_sems.at[r, 2 * u + j],
                    far[r],
                ).wait_recv()
                value = value + far_take[r, 2 * u + j]
            total_ref[2 * u + j, core, bit_x, bit_y, on_line(line), :] = value.astype(BF16)
        place = total_ref.at[pl.ds(2 * u, 2), core, bit_x, bit_y, on_line(line), :]
        for _, device in peers:
            push(place, place, sent_sems.at[u, 2], gather_sems.at[u, 0], device)

    def spread_on(u, slot, place, device):
        push(place, place, sent_sems.at[u, 2], gather_sems.at[u, slot], device)

    def stage5(u):
        three = total_ref.at[pl.ds(2 * u, 2), core, bit_x, bit_y, pl.ds(0, 3 * piece), :]
        settled(three, gather_sems.at[u, 0])
        for j, device in ((0, to_y), (1, to_x)):
            spread_on(u, 1 + j, total_ref.at[2 * u + j, core, bit_x, bit_y], device)

    def stage6(u):
        for j, at, device in ((0, (bit_x,), to_x), (1, (slice(None), bit_y), to_y)):
            settled(total_ref.at[2 * u + j, core, bit_x, bit_y], gather_sems.at[u, 1 + j])
            spread_on(u, 3 + j, total_ref.at[(2 * u + j, core) + at], device)

    def stage7(u):
        for j in range(2):
            settled(total_ref.at[2 * u + j, core, bit_x], gather_sems.at[u, 3 + j])
        spread_on(u, 5, total_ref.at[pl.ds(2 * u, 2), core], other)

    outs = []

    def leave(source, target, at):
        outs.append(pltpu.make_async_copy(source, target, out_sems.at[at]))
        outs[-1].start()

    def stage8(u):
        settled(total_ref.at[pl.ds(2 * u, 2), core], gather_sems.at[u, 5])
        leave(total_ref.at[pl.ds(2 * u, 2)], total_hbm.at[pl.ds(2 * u, 2)], u)

    def all_sent(u):
        rows_sent = 2 * (4 + 2 + 1) * depth + 6 * piece
        by_lanes = glow_ref.at[pl.ds(0, rows_sent // 2), pl.ds(0, 2 * width)]
        settled(by_lanes, sent_sems.at[u, 0])
        settled(by_lanes, sent_sems.at[u, 2])
        settled(enc_t_ref.at[pl.ds(0, 24), pl.ds(0, width // 2)], sent_sems.at[u, 1])

    part_rows = small_ref.shape[0] // 2

    def small_send(slot, source, device):
        flights["s", slot] = send(source, small_take.at[slot], small_sems.at[slot], device)

    def small_step(stage):
        mine = pl.ds(pl.multiple_of(core * part_rows, part_rows), part_rows)
        if stage == 0:
            theirs = pl.ds(pl.multiple_of((1 - core) * part_rows, part_rows), part_rows)
            small_send(0, small_ref.at[theirs, :], other)
        elif stage == 1:
            flights["s", 0].wait_recv()
            small_now[0] = small_ref[mine, :] + small_take[0]
            small_send(1, small_now.at[0], to_x)
        elif stage == 2:
            flights["s", 1].wait_recv()
            small_now[1] = small_now[0] + small_take[1]
            small_send(2, small_now.at[1], to_y)
        elif stage == 3:
            flights["s", 2].wait_recv()
            small_now[2] = small_now[1] + small_take[2]
            for step, (_, device) in enumerate(peers):
                small_send(3 + step, small_now.at[2], device)
        elif stage == 4:
            for step in range(3):
                flights["s", 3 + step].wait_recv()
            value = (small_now[2] + small_take[3]) + (small_take[4] + small_take[5])
            for r in range(rounds):
                small_now[3 + r] = value
                small_send(6 + r, small_now.at[3 + r], far[r])
                flights["s", 6 + r].wait_recv()
                value = value + small_take[6 + r]
            small_total_ref[mine, :] = value
            place = small_total_ref.at[mine, :]
            flights["s", "last"] = send(place, place, small_sems.at[6 + rounds], other)
        elif stage == 5:
            flights["s", "last"].wait_recv()
            leave(small_total_ref, small_total_hbm, UNITS + 1)

    def own_lanes(b):
        return pl.ds(pl.multiple_of(b * frames + core * half, half), half)

    def far_lanes(b):
        return pl.ds(pl.multiple_of(b * frames + (1 - core) * half, half), half)

    def project(source, place):
        value = source[...].reshape(utts * half, enc_w_ref.shape[0])
        enc_proj = dot(value, enc_w_ref[...]) + enc_b_ref[...].astype(F32)[None, :]
        turned = jnp.transpose(enc_proj.astype(BF16).astype(F32))
        for b in range(utts):
            enc_t_ref[:, place(b)] = turned[:, b * half : (b + 1) * half]

    load_enc_w.wait()
    load_enc.wait()
    project(enc_own_ref, own_lanes)
    load_out_w.wait()
    out_wt_ref[pl.ds(0, vocab), :] = jnp.transpose(out_w_ref[...])
    bias_ref[pl.ds(0, vocab), :] = column_of(out_b_ref[...].astype(F32)[None, :])
    small_ref[...] = jnp.zeros(small_ref.shape, F32)
    blank_ref[...] = jnp.full(blank_ref.shape, NEGATIVE_FILL, F32)
    emit_ref[...] = jnp.full(emit_ref.shape, NEGATIVE_FILL, F32)
    low_ref[pl.ds(width, 16), :] = jnp.ones((16, low_ref.shape[1]), BF16)
    spread = jnp.where(iota((width, 4), 0) % 4 == iota((width, 4), 1), 1.0, 0.0).astype(BF16)
    same_group = iota((width, width), 0) // 4 == iota((width, width), 1) // 4
    group = width // 4
    widen = jnp.where(iota((group, width), 0) == iota((group, width), 1) // 4, 1.0, 0.0).astype(BF16)
    lane_out = iota((1, width), 1) % 4
    taps = []
    for tap in range(2):
        kernel_rows = []
        for i in range(4):
            spans = dot(conv_w_ref[tap, i], widen)
            row = jnp.zeros((1, width), F32)
            for o in range(4):
                row = jnp.where(lane_out == o, spans[o : o + 1], row)
            kernel_rows.append(row)
        kernel_rows = jnp.concatenate(kernel_rows, axis=0).astype(BF16)
        taps.append(jnp.where(same_group, dot(spread, kernel_rows), 0.0).astype(BF16))

    swap_labels.wait_recv()
    swap_starts.wait_recv()
    pieces = []
    for b in range(utts):
        own = labels_own_ref[pl.ds(first + b, 1), :].astype(F32)
        theirs = labels_far_ref[pl.ds(first + b, 1), :].astype(F32)
        pieces += [jnp.where(core == 0, own, theirs), jnp.where(core == 0, theirs, own)]
    label_row = jnp.concatenate(pieces, axis=1)
    for b in range(utts):
        for place, source in ((core, starts_own_ref), (1 - core, starts_far_ref)):
            starts_ref[pl.ds(b, 1), pl.ds(pl.multiple_of(place * half, half), half)] = source[
                pl.ds(first + b, 1), :
            ]
    within = iota((1, rows), 1) % positions
    token_row = jnp.where(within == 0, 0.0, pltpu.roll(label_row, 1, 1))
    label_col = column_of(label_row)
    token_col = column_of(token_row)
    vocab_lane = iota((rows, 128), 1).astype(F32)

    def one_hot(column):
        parts = [
            jnp.where(vocab_lane + float(at) == column, 1.0, 0.0).astype(BF16)
            for at in range(0, vocab, 128)
        ]
        return jnp.concatenate(parts, axis=1)

    row_within = iota((rows, width), 0) % positions
    load_table.wait()
    emb = dot(one_hot(token_col), table_ref[...])
    emb_prev = jnp.where(row_within == 0, 0.0, pltpu.roll(emb, 1, 0))
    emb_low = emb.astype(BF16)
    prev_low = emb_prev.astype(BF16)
    conv_out = dot(prev_low, taps[0]) + dot(emb_low, taps[1])
    conv_out = conv_out + conv_b_ref[...].astype(F32)[None, :]
    mean = jnp.mean(conv_out, axis=1, keepdims=True)
    centered = conv_out - mean
    rstd = lax.rsqrt(jnp.mean(centered * centered, axis=1, keepdims=True) + NORM_EPS)
    normed = centered * rstd
    gain = gain_ref[...].astype(F32)[None, :]
    scaled = normed * gain + shift_ref[...].astype(F32)[None, :]
    sigmoid = 1.0 / (1.0 + jnp.exp(-scaled))
    hidden = scaled * sigmoid
    hidden_low = hidden.astype(BF16)
    load_dec_w.wait()
    dec_proj = dot(hidden_low, dec_w_ref[...]) + dec_b_ref[...].astype(F32)[None, :]
    dec_t_ref[...] = jnp.transpose(dec_proj).astype(BF16)

    label_hot = one_hot(label_col)
    picks = pl.ds(vocab, rows)
    out_wt_ref[picks, :] = dot(label_hot, out_wt_ref[pl.ds(0, vocab), :]).astype(BF16)
    bias_ref[picks, :] = dot(label_hot, bias_ref[pl.ds(0, vocab), :].astype(BF16))
    wide_label = wide(label_col, frames // 128)
    swap_enc.wait_recv()
    project(enc_far_ref, far_lanes)

    block = 256

    def selector(b, k):
        begin = starts_ref[pl.ds(b, 1), :] + (k + b * positions)
        return iota((rows, frames), 0) == begin

    def chunk_lanes(c):
        return pl.ds(pl.multiple_of(c * frames, frames), frames)

    def utt_lanes(c):
        return pl.ds(pl.multiple_of((c // WINDOW) * frames, frames), frames)

    def activate(c):
        hot = jnp.where(selector(c // WINDOW, c % WINDOW), 1.0, 0.0).astype(BF16)
        act = jnp.tanh(enc_t_ref[:, utt_lanes(c)] + dot(dec_t_ref[...], hot))
        act_ref[c] = act
        low_ref[pl.ds(0, width), chunk_lanes(c)] = act.astype(BF16)

    def score(c, raw_ref):
        low = low_ref[pl.ds(0, width), chunk_lanes(c)]
        raw_ref[...] = dot(out_wt_ref[...], low) + wide(bias_ref[...], frames // 128)

    def normalise(c, raw_ref):
        b = c // WINDOW
        k = c % WINDOW
        top = jnp.max(raw_ref[pl.ds(0, vocab), :], axis=0, keepdims=True)
        total = jnp.zeros((1, frames), F32)
        for v in range(0, vocab, block):
            part = jnp.exp(raw_ref[pl.ds(v, block), :] - top)
            exp_ref[c, pl.ds(v, block), :] = part
            total = total + jnp.sum(part, axis=0, keepdims=True)
        log_norm = top + jnp.log(total)
        picked = selector(b, k)
        target = jnp.where(picked, raw_ref[pl.ds(vocab, rows), :], 0.0)
        target = jnp.sum(target, axis=0, keepdims=True) - log_norm
        live = starts_ref[pl.ds(b, 1), :] + k < lengths_ref[first + b]
        here = (pl.ds(k, 1), utt_lanes(c))
        blank_ref[here] = raw_ref[pl.ds(0, 1), :] - log_norm
        emit_ref[here] = jnp.where(live, target, NEGATIVE_FILL)
        inv_ref[here] = 1.0 / total
        wide_label_ref[here] = jnp.sum(jnp.where(picked, wide_label, 0.0), axis=0, keepdims=True)

    activate(0)
    activate(1)
    score(0, raw_a_ref)

    def forward(i, carry):
        c = 2 * i
        score(c + 1, raw_b_ref)
        normalise(c, raw_a_ref)
        activate(jnp.minimum(c + 2, chunks - 1))
        score(jnp.minimum(c + 2, chunks - 1), raw_a_ref)
        normalise(c + 1, raw_b_ref)
        activate(jnp.minimum(c + 3, chunks - 1))
        return carry

    lax.fori_loop(0, chunks // 2, forward, 0)

    starts_row = jnp.concatenate([starts_ref[b : b + 1, :] for b in range(utts)], axis=1)
    lane_row = iota((1, lanes), 1)
    moved = jnp.where(lane_row % frames == 0, 0, starts_row - pltpu.roll(starts_row, 1, 1))
    scale = jnp.zeros((1, lanes), F32)
    for b in range(utts):
        scale = jnp.where(lane_row // frames == b, -cot_ref[first + b] / frames, scale)
    leaving, blank_g, emit_g = lattice(blank_ref[...], emit_ref[...], moved, scale, frames)
    blank_g_ref[...] = blank_g
    emit_g_ref[...] = emit_g
    factor_ref[...] = -(blank_g + emit_g) * inv_ref[...]
    ends = iota((8, lanes), 1)
    for b in range(utts):
        last = (ends == (b + 1) * frames - 1) & (iota((8, lanes), 0) == WINDOW - 1)
        loss_ref[b] = -jnp.sum(jnp.where(last, leaving, 0.0)) / frames

    def logits_back(v):
        ids = iota((block, frames), 0) + v
        for c in range(chunks):
            b, k = c // WINDOW, c % WINDOW
            here = (slice(k, k + 1), slice(b * frames, (b + 1) * frames))
            blank_now, emit_now, factor = blank_g_ref[here], emit_g_ref[here], factor_ref[here]
            label_now = wide_label_ref[here].astype(jnp.int32)
            other_part = jnp.where(ids == 0, blank_now, 0.0) if v == 0 else 0.0
            grad = exp_ref[c, pl.ds(v, block), :] * factor + jnp.where(
                ids == label_now, emit_now, other_part
            )
            glow_ref[pl.ds(v, block), pl.ds(c * frames, frames)] = grad.astype(BF16)

    def weight_back(v):
        total = dot_nt(low_ref[...], glow_ref[pl.ds(v, block), :])
        grads_ref[v // width, :, :, :, :, pl.ds(v % width, block)] = total[:width].reshape(
            grads_ref.shape[1:5] + (block,)
        )
        small_ref[pl.ds(13 + v // width, 1), pl.ds(v % width, block)] = total[width : width + 1]

    logits_back(0)
    for v in range(0, vocab, block):
        weight_back(v)
        if v + block < vocab:
            logits_back(v + block)

    stage0(0)

    enc_sum_ref[...] = jnp.zeros(enc_sum_ref.shape, F32)
    dec_sum_ref[...] = jnp.zeros(dec_sum_ref.shape, F32)

    def pull(c, back_ref):
        back_ref[pl.ds(0, width), :] = dot(out_w_ref[...], glow_ref[:, chunk_lanes(c)])

    def settle(c, back_ref):
        act = act_ref[c]
        grad = back_ref[pl.ds(0, width), :] * (1.0 - act * act)
        enc_sum_ref[:, utt_lanes(c)] += grad
        hot = jnp.where(selector(c // WINDOW, c % WINDOW), 1.0, 0.0).astype(BF16)
        both = dot_nt(jnp.concatenate(halves(grad), axis=0), hot)
        dec_sum_ref[...] += both[:width] + both[width:]

    def backward(i, carry):
        c = 2 * i
        pull(c + 1, raw_b_ref)
        settle(c, raw_a_ref)
        pull(jnp.minimum(c + 2, chunks - 1), raw_a_ref)
        settle(c + 1, raw_b_ref)
        return carry

    pull(0, raw_a_ref)
    lax.fori_loop(0, chunks // 2, backward, 0)
    stage1(0)

    enc_b_grad = jnp.zeros((1, width), F32)
    enc_w_grad = jnp.zeros((enc_w_ref.shape[0], width), F32)
    for source, place, target in (
        (enc_far_ref, far_lanes, enc_g_send_ref),
        (enc_own_ref, own_lanes, enc_g_own_ref),
    ):
        enc_g = jnp.concatenate([enc_sum_ref[:, place(b)] for b in range(utts)], axis=1)
        enc_g = jnp.transpose(enc_g).astype(BF16)
        target[...] = enc_g.reshape(utts, half, width)
        value = source[...].reshape(utts * half, enc_w_ref.shape[0])
        enc_w_grad = enc_w_grad + dot(jnp.transpose(value), enc_g)
        enc_b_grad = enc_b_grad + jnp.sum(enc_g.astype(F32), axis=0, keepdims=True)
    grads_ref[2] = enc_w_grad.reshape(grads_ref.shape[1:])
    enc_copy = send(enc_g_send_ref, enc_g_far_hbm, enc_sems, other)
    leave(enc_g_own_ref, enc_g_own_hbm, UNITS)

    dec_g = jnp.transpose(dec_sum_ref[...]).astype(BF16)
    dec_b_grad = jnp.sum(dec_g.astype(F32), axis=0, keepdims=True)
    grads_ref[3] = dot(jnp.transpose(hidden).astype(BF16), dec_g).reshape(grads_ref.shape[1:])
    stage0(1)
    hidden_grad = dot_nt(dec_g, dec_w_ref[...])
    scaled_grad = hidden_grad * (sigmoid * (1.0 + scaled * (1.0 - sigmoid)))
    gain_grad = jnp.sum(scaled_grad * normed, axis=0, keepdims=True)
    shift_grad = jnp.sum(scaled_grad, axis=0, keepdims=True)
    normed_grad = scaled_grad * gain
    conv_grad = rstd * (
        normed_grad
        - jnp.mean(normed_grad, axis=1, keepdims=True)
        - normed * jnp.mean(normed_grad * normed, axis=1, keepdims=True)
    )
    high, rest = halves(conv_grad)
    prev_grad = dot_nt(high, taps[0]) + dot_nt(rest, taps[0])
    emb_grad = dot_nt(high, taps[1]) + dot_nt(rest, taps[1])
    emb_grad = emb_grad + jnp.where(
        row_within == positions - 1, 0.0, pltpu.roll(prev_grad, rows - 1, 0)
    )
    high, rest = halves(emb_grad)
    token_hot_t = jnp.where(
        iota((vocab, rows), 0) == token_row.astype(jnp.int32), 1.0, 0.0
    ).astype(BF16)
    for part in range(vocab // width):
        hot = token_hot_t[part * width : (part + 1) * width]
        table_grad = dot(hot, high) + dot(hot, rest)
        grads_ref[4 + part] = table_grad.reshape(grads_ref.shape[1:])
    stage0(2)

    conv_b_grad = jnp.sum(conv_grad, axis=0, keepdims=True)
    turned = halves(jnp.transpose(conv_grad))
    fold = jnp.where(iota((8, width), 1) % 4 == iota((8, width), 0), 1.0, 0.0).astype(BF16)
    for tap, source in enumerate((prev_low, emb_low)):
        outer = jnp.where(same_group, dot(turned[0], source) + dot(turned[1], source), 0.0)
        high, rest = halves(outer)
        folded = dot(fold, high) + dot(fold, rest)
        small_ref[pl.ds(4 * tap, 4), :] = folded[:4]
    for at, value in enumerate((conv_b_grad, gain_grad, shift_grad, dec_b_grad, enc_b_grad)):
        small_ref[pl.ds(8 + at, 1), :] = value

    small_step(0)
    order = (
        ((2, 0), (1, 1), (3, 0), (1, 2)),
        ((2, 1), (4, 0), (2, 2), (3, 1)),
        ((3, 2), (5, 0), (4, 1)),
        ((6, 0), (4, 2), (5, 1)),
        ((7, 0), (5, 2), (6, 1)),
        ((6, 2), (7, 1), (7, 2), (8, 1), (8, 0), (8, 2)),
    )
    stages = (stage0, stage1, stage2, stage3, stage4, stage5, stage6, stage7, stage8)
    for at, steps in enumerate(order):
        for stage, u in steps:
            stages[stage](u)
        if at < 5:
            small_step(at + 1)
    for u in range(UNITS):
        all_sent(u)
    enc_copy.wait_recv()
    for copy in pending:
        copy.wait_send()
    for copy in outs:
        copy.wait()


def finish_kernel(
    share,
    loss_in_ref,
    small_hbm,
    total_hbm,
    enc_g_own_hbm,
    enc_g_far_hbm,
    enc_w_hbm,
    loss_ref,
    enc_grad_hbm,
    table_hbm,
    conv_w_hbm,
    conv_b_hbm,
    gain_hbm,
    shift_hbm,
    dec_w_hbm,
    dec_b_hbm,
    enc_w_grad_hbm,
    enc_b_hbm,
    out_w_hbm,
    out_b_hbm,
    enc_grad_ref,
    table_ref,
    dec_w_ref,
    enc_w_grad_ref,
    out_w_ref,
    total_ref,
    enc_g_own_ref,
    enc_g_far_ref,
    enc_w_ref,
    small_ref,
    conv_w_ref,
    vector_ref,
    out_b_ref,
    load_sems,
    sems,
):
    core = lax.axis_index("au")
    width = enc_w_ref.shape[1]
    loads = []
    for i in range(BLOCKS):
        loads.append((total_hbm.at[i], total_ref.at[i]))
    loads += [
        (enc_w_hbm, enc_w_ref),
        (enc_g_own_hbm, enc_g_own_ref),
        (enc_g_far_hbm, enc_g_far_ref),
        (small_hbm, small_ref),
    ]
    loads = [
        pltpu.make_async_copy(source, target, load_sems.at[at])
        for at, (source, target) in enumerate(loads)
    ]
    for load in loads:
        load.start()
    copies = []

    def leave(source, target):
        copies.append(pltpu.make_async_copy(source, target, sems.at[len(copies)]))
        copies[-1].start()

    for b in range(share):
        loss_ref[b] = loss_in_ref[b]
    every = pl.ds(0, width)
    for i, target, home, where in (
        (0, out_w_ref, out_w_hbm, (every, pl.ds(0, width))),
        (1, out_w_ref, out_w_hbm, (every, pl.ds(width, width))),
        (2, enc_w_grad_ref, enc_w_grad_hbm, (every, every)),
        (3, dec_w_ref, dec_w_hbm, (every, every)),
        (4, table_ref, table_hbm, (pl.ds(0, width), every)),
        (5, table_ref, table_hbm, (pl.ds(width, width), every)),
    ):
        loads[i].wait()
        target[where] = total_ref[i].astype(F32).reshape(width, width)
        leave(target.at[where], home.at[where])
    loads[BLOCKS].wait()
    for at, source, place in (
        (BLOCKS + 1, enc_g_own_ref, core),
        (BLOCKS + 2, enc_g_far_ref, 1 - core),
    ):
        loads[at].wait()
        utts, half, _ = source.shape
        grad = dot_nt(source[...].reshape(utts * half, width), enc_w_ref[...])
        mine = pl.ds(place * share, share)
        enc_grad_ref[mine] = grad.reshape(utts, half, enc_w_ref.shape[0])
        leave(enc_grad_ref.at[mine], enc_grad_hbm.at[mine])
    loads[BLOCKS + 3].wait()
    for at, home in enumerate((conv_b_hbm, gain_hbm, shift_hbm, dec_b_hbm, enc_b_hbm)):
        vector_ref[at, :] = small_ref[8 + at, :]
    out_b_ref[pl.ds(0, width)] = small_ref[13, :]
    out_b_ref[pl.ds(width, width)] = small_ref[14, :]
    for at, home in enumerate((conv_b_hbm, gain_hbm, shift_hbm, dec_b_hbm, enc_b_hbm)):
        leave(vector_ref.at[at], home)
    leave(out_b_ref, out_b_hbm)
    group = width // 4
    high, rest = halves(small_ref[:8, :])
    last = (small_ref[:8, :] - high.astype(F32) - rest.astype(F32)).astype(BF16)
    for i in range(4):
        take = iota((width, group), 0) == 4 * iota((width, group), 1) + i
        take = jnp.where(take, 1.0, 0.0).astype(BF16)
        picked = dot(high, take) + dot(rest, take) + dot(last, take)
        for tap in range(2):
            conv_w_ref[tap, i] = picked[4 * tap : 4 * tap + 4]
    leave(conv_w_ref, conv_w_hbm)
    for copy in copies:
        copy.wait()


def on_device(
    item_count,
    encoder_out,
    labels,
    lengths,
    starts,
    loss_cot,
    embed_table,
    conv_weight,
    conv_bias,
    norm_gain,
    norm_bias,
    dec_weight,
    dec_bias,
    enc_weight,
    enc_bias,
    out_weight,
    out_bias,
):
    utt_count, half, enc_dim = encoder_out.shape
    dec_dim = embed_table.shape[1]
    width, vocab = out_weight.shape
    share = utt_count // 2
    frames = 2 * half
    pairs = share * frames * WINDOW
    rows = share * 2 * labels.shape[1]
    lanes = share * frames
    chunks = share * WINDOW
    rounds = (item_count // 16).bit_length() - 1
    split = (2, 2, 2, width // 8, width)
    deep = max(rounds, 1)
    vmem = pl.BlockSpec(memory_space=pltpu.VMEM)
    smem = pl.BlockSpec(memory_space=pltpu.SMEM)
    anywhere = pl.BlockSpec(memory_space=pl.ANY)
    struct = jax.ShapeDtypeStruct
    mem = pltpu.VMEM
    dma = pltpu.SemaphoreType.DMA
    code = jnp.int16

    losses, enc_g_own, enc_g_far, small, totals = pl.pallas_call(
        functools.partial(main_kernel, share, rounds),
        out_shape=(
            struct((share,), F32),
            struct((share, half, width), BF16),
            struct((share, half, width), BF16),
            struct((16, width), F32),
            struct((BLOCKS,) + split, BF16),
        ),
        in_specs=[smem] * 2 + [vmem] * 9 + [anywhere] * 5,
        out_specs=(smem,) + (anywhere,) * 4,
        scratch_shapes=[
            mem(labels.shape, labels.dtype),
            mem(starts.shape, starts.dtype),
            mem((share, half, enc_dim), BF16),
            mem((share, half, enc_dim), BF16),
            mem(embed_table.shape, BF16),
            mem(dec_weight.shape, BF16),
            mem(enc_weight.shape, BF16),
            mem(out_weight.shape, BF16),
            mem((vocab + rows, width), BF16),
            mem((vocab + rows, 128), F32),
            mem((width, rows), BF16),
            mem((width, lanes), F32),
            mem((vocab + rows, frames), F32),
            mem((vocab + rows, frames), F32),
            mem((chunks, vocab, frames), F32),
            mem((chunks, width, frames), F32),
            mem((width + 16, pairs), BF16),
            mem((vocab, pairs), BF16),
        ]
        + [mem((8, lanes), F32)] * 7
        + [
            mem((width, lanes), F32),
            mem((width, rows), F32),
            mem((8, frames), jnp.int32),
            mem((BLOCKS,) + split, F32),
            mem((16, width), F32),
            mem((share, half, width), BF16),
            mem((share, half, width), BF16),
            mem((BLOCKS,) + split, BF16),
            mem((16, width), F32),
        ]
        + [
            mem((UNITS, 2) + split[1:], code),
            mem((UNITS, 2) + split[2:], code),
            mem((UNITS, 2) + split[3:], code),
        ]
        * 2
        + [
            mem((UNITS, 2, split[3], width), code),
            mem((UNITS, 3, 2, split[3] // 4, width), code),
            mem((UNITS, 6, 2, 1, width), F32),
            mem((UNITS, 6, 2, 1, width), F32),
            mem((3 + rounds, 8, width), F32),
            mem((6 + rounds, 8, width), F32),
            mem((deep, BLOCKS, split[3] // 4, width), F32),
            mem((deep, BLOCKS, split[3] // 4, width), F32),
            dma((5,)),
            dma((3, 2)),
            dma((UNITS, 6)),
            dma((UNITS, 6)),
            dma((UNITS, 6)),
            dma((UNITS, 3)),
            dma((7 + rounds, 2)),
            dma((deep, BLOCKS, 2)),
            dma((2,)),
            dma((UNITS + 2,)),
        ],
        compiler_params=pltpu.CompilerParams(
            collective_id=0, has_side_effects=True, vmem_limit_bytes=58 * MIB
        ),
        name="main",
    )(
        lengths,
        loss_cot,
        labels,
        starts,
        jnp.transpose(conv_weight, (0, 2, 3, 1)),
        conv_bias,
        norm_gain,
        norm_bias,
        dec_bias,
        enc_bias,
        out_bias,
        encoder_out,
        embed_table,
        dec_weight,
        enc_weight,
        out_weight,
    )

    vector = struct((width,), F32)
    square = struct((width, width), F32)
    outs = pl.pallas_call(
        functools.partial(finish_kernel, share),
        out_shape=(
            struct((share,), F32),
            struct(encoder_out.shape, F32),
            struct(embed_table.shape, F32),
            struct((2, 4, 4, dec_dim // 4), F32),
            vector,
            vector,
            vector,
            square,
            vector,
            square,
            vector,
            struct(out_weight.shape, F32),
            struct(out_bias.shape, F32),
        ),
        in_specs=[smem] + [anywhere] * 5,
        out_specs=(smem,) + (anywhere,) * 12,
        scratch_shapes=[
            mem(encoder_out.shape, F32),
            mem(embed_table.shape, F32),
            mem((width, width), F32),
            mem((width, width), F32),
            mem(out_weight.shape, F32),
            mem((BLOCKS,) + split, BF16),
            mem((share, half, width), BF16),
            mem((share, half, width), BF16),
            mem(enc_weight.shape, BF16),
            mem((16, width), F32),
            mem((2, 4, 4, dec_dim // 4), F32),
            mem((8, width), F32),
            mem(out_bias.shape, F32),
            dma((BLOCKS + 4,)),
            dma((BLOCKS + 9,)),
        ],
        compiler_params=pltpu.CompilerParams(vmem_limit_bytes=62 * MIB),
        name="finish",
    )(losses, small, totals, enc_g_own, enc_g_far, enc_weight)
    return outs[:3] + (jnp.transpose(outs[3], (0, 3, 1, 2)),) + outs[4:]


def solution(mesh):
    in_specs = (
        P("items", "au", None),
        P("items", "au"),
        P("items"),
        P("items", "au"),
        P("items"),
    ) + (P(),) * 11
    out_specs = (P(("items", "au")), P("items", "au", None)) + (P(),) * 11
    return jax.shard_map(
        functools.partial(on_device, mesh.shape["items"]),
        mesh=mesh,
        in_specs=in_specs,
        out_specs=out_specs,
        check_vma=False,
    )
```

```python
import functools

import jax
import jax.numpy as jnp
from jax import lax
from jax.experimental import pallas as pl
from jax.experimental.pallas import tpu as pltpu
from jax.sharding import PartitionSpec as P

WINDOW = 5
NEGATIVE_FILL = -1e30
NORM_EPS = 1e-05
F32 = jnp.float32
BF16 = jnp.bfloat16
MIB = 1 << 20
MESH = pl.DeviceIdType.MESH


def dot(a, b):
    return lax.dot_general(a, b, (((1,), (0,)), ((), ())), preferred_element_type=F32)


def dot_nt(a, b):
    return lax.dot_general(a, b, (((1,), (1,)), ((), ())), preferred_element_type=F32)


def halves(x):
    high = x.astype(BF16)
    return high, (x - high.astype(F32)).astype(BF16)


def iota(shape, dim):
    return lax.broadcasted_iota(jnp.int32, shape, dim)


def column_of(row):
    return jnp.transpose(jnp.broadcast_to(row, (128, row.shape[1])))


def shift_rows(x, moved):
    out = x
    for step in (1, 2, 3):
        out = jnp.where(moved == step, pltpu.roll(x, step, 0), out)
    return out


def lattice(blank, emit, moved, scale, frames):
    lanes = blank.shape[1]
    row = iota((8, lanes), 0)
    lane = iota((8, lanes), 1) % frames
    window_row = row < WINDOW
    before = jnp.where(
        lane == 0, jnp.where(row == 0, 0.0, NEGATIVE_FILL), pltpu.roll(blank, 1, 1)
    )
    path = jnp.where(row == 0, 0.0, NEGATIVE_FILL)
    prefix = []
    for k in range(WINDOW):
        if k:
            path = jnp.where(
                row == k, 0.0, jnp.where(row < k, path + emit[k - 1 : k], NEGATIVE_FILL)
            )
        prefix.append(shift_rows(path, moved) + before)
    reach = 1
    while reach < frames:
        earlier = [pltpu.roll(column, reach, 1) for column in prefix]
        joined = []
        for k in range(WINDOW):
            terms = [earlier[i] + prefix[k][i : i + 1] for i in range(WINDOW)]
            top = functools.reduce(jnp.maximum, terms)
            total = functools.reduce(jnp.add, [jnp.exp(term - top) for term in terms])
            joined.append(top + jnp.log(total))
        prefix = [jnp.where(lane >= reach, new, old) for new, old in zip(joined, prefix)]
        reach *= 2
    alpha = jnp.concatenate(
        [column[:1] for column in prefix] + [jnp.full((8 - WINDOW, lanes), NEGATIVE_FILL, F32)], axis=0
    )
    leaving = alpha + blank
    arrived = pltpu.roll(leaving, 1, 1)
    entry = arrived
    for step in (1, 2, 3):
        entry = jnp.where(moved == step, pltpu.roll(arrived, 8 - step, 0), entry)
    entry = jnp.where(lane == 0, jnp.where(row == 0, 0.0, NEGATIVE_FILL), entry)
    lead = pltpu.roll(alpha + emit, 1, 0) - entry
    from_emit = jnp.where(window_row & (row > 0), 1.0 / (1.0 + jnp.exp(-lead)), 0.0)
    from_entry = jnp.where(row == 0, 1.0, jnp.where(window_row, 1.0 / (1.0 + jnp.exp(lead)), 0.0))
    suffix = []
    flow = jnp.zeros((8, lanes), F32)
    for n in range(WINDOW):
        flow = jnp.where(row == n, from_entry, flow * from_emit[n : n + 1])
        suffix.append(jnp.where(window_row, shift_rows(flow, moved), 0.0))
    reach = 1
    while reach < frames:
        later = [pltpu.roll(column, lanes - reach, 1) for column in suffix]
        joined = []
        for n in range(WINDOW):
            terms = [suffix[i] * later[n][i : i + 1] for i in range(WINDOW)]
            joined.append(functools.reduce(jnp.add, terms))
        suffix = [
            jnp.where(lane < frames - reach, new, old) for new, old in zip(joined, suffix)
        ]
        reach *= 2
    outward = jnp.where(
        lane == frames - 1,
        jnp.where(row == WINDOW - 1, 1.0, 0.0),
        pltpu.roll(suffix[WINDOW - 1], lanes - 1, 1),
    )
    state = jnp.zeros((1, lanes), F32)
    upward = [None] * WINDOW
    for k in range(WINDOW - 1, -1, -1):
        upward[k] = state
        state = outward[k : k + 1] + state
        if k:
            state = state * from_emit[k : k + 1]
    emitted = jnp.concatenate(upward + [jnp.zeros((8 - WINDOW, lanes), F32)], axis=0)
    return leaving, outward * scale, emitted * scale


BLOCKS = 6
UNITS = BLOCKS // 2
LEVELS = 32000.0

WHOLE = 12582912.0


def coded(value):
    top = jnp.maximum(jnp.max(jnp.abs(value), axis=0, keepdims=True), 1e-30)
    code = (value * (LEVELS / top) + WHOLE) - WHOLE
    return code.astype(jnp.int32).astype(jnp.int16), top * (1.0 / LEVELS)


def decoded(code, scale):
    return code.astype(jnp.int32).astype(F32) * scale


def wide(row, count):
    return jnp.concatenate([row] * count, axis=1)


def main_kernel(
    share,
    rounds,
    lengths_ref,
    cot_ref,
    labels_own_ref,
    starts_own_ref,
    conv_w_ref,
    conv_b_ref,
    gain_ref,
    shift_ref,
    dec_b_ref,
    enc_b_ref,
    out_b_ref,
    enc_hbm,
    table_hbm,
    dec_w_hbm,
    enc_w_hbm,
    out_w_hbm,
    loss_ref,
    enc_g_own_hbm,
    enc_g_far_hbm,
    small_total_hbm,
    total_hbm,
    labels_far_ref,
    starts_far_ref,
    enc_own_ref,
    enc_far_ref,
    table_ref,
    dec_w_ref,
    enc_w_ref,
    out_w_ref,
    out_wt_ref,
    bias_ref,
    dec_t_ref,
    enc_t_ref,
    raw_a_ref,
    raw_b_ref,
    exp_ref,
    act_ref,
    low_ref,
    glow_ref,
    blank_ref,
    emit_ref,
    inv_ref,
    wide_label_ref,
    blank_g_ref,
    emit_g_ref,
    factor_ref,
    enc_sum_ref,
    dec_sum_ref,
    starts_ref,
    grads_ref,
    small_ref,
    enc_g_send_ref,
    enc_g_own_ref,
    total_ref,
    small_total_ref,
    send_core,
    send_one,
    send_two,
    take_core,
    take_one,
    take_two,
    send_line,
    take_line,
    send_scale,
    take_scale,
    small_now,
    small_take,
    far_now,
    far_take,
    load_sems,
    swap_sems,
    code_sems,
    scale_sems,
    gather_sems,
    sent_sems,
    small_sems,
    far_sems,
    enc_sems,
    out_sems,
):
    core = lax.axis_index("au")
    item = lax.axis_index("items")
    utts = share
    half = starts_own_ref.shape[1]
    positions = 2 * labels_own_ref.shape[1]
    frames = 2 * half
    width, vocab = out_w_ref.shape
    rows = utts * positions
    lanes = utts * frames
    chunks = utts * WINDOW
    first = core * share

    loads = []
    for at, (source, target) in enumerate(
        (
            (enc_w_hbm, enc_w_ref),
            (enc_hbm.at[pl.ds(first, share)], enc_own_ref),
            (out_w_hbm, out_w_ref),
            (table_hbm, table_ref),
            (dec_w_hbm, dec_w_ref),
        )
    ):
        loads.append(pltpu.make_async_copy(source, target, load_sems.at[at]))
        loads[-1].start()
    load_enc_w, load_enc, load_out_w, load_table, load_dec_w = loads

    bit_x = item % 2
    bit_y = (item // 2) % 2
    line = (item // 4) % 4
    base = item - line * 4
    other = {"items": item, "au": 1 - core}
    to_x = {"items": item + 1 - 2 * bit_x, "au": core}
    to_y = {"items": item + 2 - 4 * bit_y, "au": core}
    peers = []
    for step in (1, 2, 3):
        low = line % 2
        high = line // 2
        low = 1 - low if step % 2 else low
        high = 1 - high if step // 2 else high
        peers.append((low + 2 * high, {"items": base + 4 * (low + 2 * high), "au": core}))
    far = []
    for r in range(rounds):
        bit = (item // (16 << r)) % 2
        far.append({"items": item + (16 << r) * (1 - 2 * bit), "au": core})
    everyone = [other, to_x, to_y] + [peer for _, peer in peers] + far

    barrier = pltpu.get_barrier_semaphore()
    for device in everyone:
        pl.semaphore_signal(barrier, inc=1, device_id=device, device_id_type=MESH)
    pl.semaphore_wait(barrier, len(everyone))

    pending = []

    def send(source, target, sems, device):
        copy = pltpu.make_async_remote_copy(
            src_ref=source,
            dst_ref=target,
            send_sem=sems.at[0],
            recv_sem=sems.at[1],
            device_id=device,
            device_id_type=MESH,
        )
        copy.start()
        pending.append(copy)
        return copy

    def push(source, target, sent, landed, device):
        pltpu.make_async_remote_copy(
            src_ref=source,
            dst_ref=target,
            send_sem=sent,
            recv_sem=landed,
            device_id=device,
            device_id_type=MESH,
        ).start()

    def settled(ref, sem):
        pltpu.make_async_copy(ref, ref, sem).wait()

    swap_labels = send(labels_own_ref, labels_far_ref, swap_sems.at[0], other)
    swap_starts = send(starts_own_ref, starts_far_ref, swap_sems.at[1], other)
    swap_enc = send(
        enc_hbm.at[pl.ds((1 - core) * share, share)], enc_far_ref, swap_sems.at[2], other
    )

    flights = {}
    depth = grads_ref.shape[4]
    piece = depth // 4

    def on_line(place):
        return pl.ds(pl.multiple_of(place * piece, piece), piece)

    def pack(value, code_ref, scale_ref):
        value = value.reshape(-1, width)
        code, scale = coded(value)
        code_ref[...] = code.reshape(code_ref.shape)
        scale_ref[...] = scale

    def unpack(code_ref, scale_ref):
        return decoded(code_ref[...], scale_ref[...])

    def ship(u, slot, source, target, scale_at, device):
        push(source, target, sent_sems.at[u, 0], code_sems.at[u, slot], device)
        push(
            send_scale.at[(u,) + scale_at],
            take_scale.at[(u,) + scale_at],
            sent_sems.at[u, 1],
            scale_sems.at[u, slot],
            device,
        )

    def landed(u, slot, target, scale_at):
        settled(target, code_sems.at[u, slot])
        settled(take_scale.at[(u,) + scale_at], scale_sems.at[u, slot])

    def held(j, u):
        return grads_ref.at[2 * u + j, core]

    def stage0(u):
        for j in range(2):
            pack(grads_ref[2 * u + j, 1 - core], send_core.at[u, j], send_scale.at[u, 0, j])
        ship(u, 0, send_core.at[u], take_core.at[u], (0,), other)

    def stage1(u):
        ways = (
            (0, (1 - bit_x,), (bit_x,), to_x),
            (1, (slice(None), 1 - bit_y), (slice(None), bit_y), to_y),
        )
        landed(u, 0, take_core.at[u], (0,))

        def part(j, at):
            return held(j, u)[at] + decoded(take_core[(u, j) + at], take_scale[u, 0, j])

        for j, away, _, _ in ways:
            pack(part(j, away), send_one.at[u, j], send_scale.at[u, 1, j])
        for j, _, _, device in ways:
            ship(u, 1 + j, send_one.at[u, j], take_one.at[u, j], (1, j), device)
        for j, _, keep, _ in ways:
            held(j, u)[keep] = part(j, keep)

    def stage2(u):
        ways = (
            (0, (bit_x, 1 - bit_y), bit_y, to_y),
            (1, (1 - bit_x, bit_y), bit_x, to_x),
        )
        for j in range(2):
            landed(u, 1 + j, take_one.at[u, j], (1, j))
        for j, away, here, _ in ways:
            value = decoded(take_one[u, j, 1 - here], take_scale[u, 1, j])
            pack(held(j, u)[away] + value, send_two.at[u, j], send_scale.at[u, 2, j])
        for j, _, _, device in ways:
            ship(u, 3 + j, send_two.at[u, j], take_two.at[u, j], (2, j), device)
        for j, _, here, _ in ways:
            held(j, u)[bit_x, bit_y] += decoded(take_one[u, j, here], take_scale[u, 1, j])

    def stage3(u):
        for j in range(2):
            landed(u, 3 + j, take_two.at[u, j], (2, j))
        for j in range(2):
            value = held(j, u)[bit_x, bit_y] + unpack(take_two.at[u, j], take_scale.at[u, 2, j])
            pack(value, send_line.at[u, j], send_scale.at[u, 3, j])
            held(j, u)[bit_x, bit_y] = value
        for step, (place, device) in enumerate(peers):
            push(
                send_line.at[u, :, on_line(place), :],
                take_line.at[u, step],
                sent_sems.at[u, 0],
                code_sems.at[u, 5],
                device,
            )
            push(
                send_scale.at[u, 3],
                take_scale.at[u, 3 + step],
                sent_sems.at[u, 1],
                scale_sems.at[u, 5],
                device,
            )

    def stage4(u):
        landed(u, 5, take_line.at[u], (pl.ds(3, 3),))
        for j in range(2):
            value = held(j, u)[bit_x, bit_y, on_line(line), :]
            for step in range(3):
                value = value + unpack(take_line.at[u, step, j], take_scale.at[u, 3 + step, j])
            for r in range(rounds):
                far_now[r, 2 * u + j] = value
                send(
                    far_now.at[r, 2 * u + j],
                    far_take.at[r, 2 * u + j],
                    far_sems.at[r, 2 * u + j],
                    far[r],
                ).wait_recv()
                value = value + far_take[r, 2 * u + j]
            total_ref[2 * u + j, core, bit_x, bit_y, on_line(line), :] = value.astype(BF16)
        place = total_ref.at[pl.ds(2 * u, 2), core, bit_x, bit_y, on_line(line), :]
        for _, device in peers:
            push(place, place, sent_sems.at[u, 2], gather_sems.at[u, 0], device)

    def spread_on(u, slot, place, device):
        push(place, place, sent_sems.at[u, 2], gather_sems.at[u, slot], device)

    def stage5(u):
        three = total_ref.at[pl.ds(2 * u, 2), core, bit_x, bit_y, pl.ds(0, 3 * piece), :]
        settled(three, gather_sems.at[u, 0])
        for j, device in ((0, to_y), (1, to_x)):
            spread_on(u, 1 + j, total_ref.at[2 * u + j, core, bit_x, bit_y], device)

    def stage6(u):
        for j, at, device in ((0, (bit_x,), to_x), (1, (slice(None), bit_y), to_y)):
            settled(total_ref.at[2 * u + j, core, bit_x, bit_y], gather_sems.at[u, 1 + j])
            spread_on(u, 3 + j, total_ref.at[(2 * u + j, core) + at], device)

    def stage7(u):
        for j in range(2):
            settled(total_ref.at[2 * u + j, core, bit_x], gather_sems.at[u, 3 + j])
        spread_on(u, 5, total_ref.at[pl.ds(2 * u, 2), core], other)

    outs = []

    def leave(source, target, at):
        outs.append(pltpu.make_async_copy(source, target, out_sems.at[at]))
        outs[-1].start()

    def stage8(u):
        settled(total_ref.at[pl.ds(2 * u, 2), core], gather_sems.at[u, 5])
        leave(total_ref.at[pl.ds(2 * u, 2)], total_hbm.at[pl.ds(2 * u, 2)], u)

    def all_sent(u):
        rows_sent = 2 * (4 + 2 + 1) * depth + 6 * piece
        by_lanes = glow_ref.at[pl.ds(0, rows_sent // 2), pl.ds(0, 2 * width)]
        settled(by_lanes, sent_sems.at[u, 0])
        settled(by_lanes, sent_sems.at[u, 2])
        settled(enc_t_ref.at[pl.ds(0, 24), pl.ds(0, width // 2)], sent_sems.at[u, 1])

    part_rows = small_ref.shape[0] // 2

    def small_send(slot, source, device):
        flights["s", slot] = send(source, small_take.at[slot], small_sems.at[slot], device)

    def small_step(stage):
        mine = pl.ds(pl.multiple_of(core * part_rows, part_rows), part_rows)
        if stage == 0:
            theirs = pl.ds(pl.multiple_of((1 - core) * part_rows, part_rows), part_rows)
            small_send(0, small_ref.at[theirs, :], other)
        elif stage == 1:
            flights["s", 0].wait_recv()
            small_now[0] = small_ref[mine, :] + small_take[0]
            small_send(1, small_now.at[0], to_x)
        elif stage == 2:
            flights["s", 1].wait_recv()
            small_now[1] = small_now[0] + small_take[1]
            small_send(2, small_now.at[1], to_y)
        elif stage == 3:
            flights["s", 2].wait_recv()
            small_now[2] = small_now[1] + small_take[2]
            for step, (_, device) in enumerate(peers):
                small_send(3 + step, small_now.at[2], device)
        elif stage == 4:
            for step in range(3):
                flights["s", 3 + step].wait_recv()
            value = (small_now[2] + small_take[3]) + (small_take[4] + small_take[5])
            for r in range(rounds):
                small_now[3 + r] = value
                small_send(6 + r, small_now.at[3 + r], far[r])
                flights["s", 6 + r].wait_recv()
                value = value + small_take[6 + r]
            small_total_ref[mine, :] = value
            place = small_total_ref.at[mine, :]
            flights["s", "last"] = send(place, place, small_sems.at[6 + rounds], other)
        elif stage == 5:
            flights["s", "last"].wait_recv()
            leave(small_total_ref, small_total_hbm, UNITS + 1)

    def own_lanes(b):
        return pl.ds(pl.multiple_of(b * frames + core * half, half), half)

    def far_lanes(b):
        return pl.ds(pl.multiple_of(b * frames + (1 - core) * half, half), half)

    def project(source, place):
        value = source[...].reshape(utts * half, enc_w_ref.shape[0])
        enc_proj = dot(value, enc_w_ref[...]) + enc_b_ref[...].astype(F32)[None, :]
        turned = jnp.transpose(enc_proj.astype(BF16).astype(F32))
        for b in range(utts):
            enc_t_ref[:, place(b)] = turned[:, b * half : (b + 1) * half]

    load_enc_w.wait()
    load_enc.wait()
    project(enc_own_ref, own_lanes)
    load_out_w.wait()
    out_wt_ref[pl.ds(0, vocab), :] = jnp.transpose(out_w_ref[...])
    bias_ref[pl.ds(0, vocab), :] = column_of(out_b_ref[...].astype(F32)[None, :])
    small_ref[...] = jnp.zeros(small_ref.shape, F32)
    blank_ref[...] = jnp.full(blank_ref.shape, NEGATIVE_FILL, F32)
    emit_ref[...] = jnp.full(emit_ref.shape, NEGATIVE_FILL, F32)
    low_ref[pl.ds(width, 16), :] = jnp.ones((16, low_ref.shape[1]), BF16)
    spread = jnp.where(iota((width, 4), 0) % 4 == iota((width, 4), 1), 1.0, 0.0).astype(BF16)
    same_group = iota((width, width), 0) // 4 == iota((width, width), 1) // 4
    group = width // 4
    widen = jnp.where(iota((group, width), 0) == iota((group, width), 1) // 4, 1.0, 0.0).astype(BF16)
    lane_out = iota((1, width), 1) % 4
    taps = []
    for tap in range(2):
        kernel_rows = []
        for i in range(4):
            spans = dot(conv_w_ref[tap, i], widen)
            row = jnp.zeros((1, width), F32)
            for o in range(4):
                row = jnp.where(lane_out == o, spans[o : o + 1], row)
            kernel_rows.append(row)
        kernel_rows = jnp.concatenate(kernel_rows, axis=0).astype(BF16)
        taps.append(jnp.where(same_group, dot(spread, kernel_rows), 0.0).astype(BF16))

    swap_labels.wait_recv()
    swap_starts.wait_recv()
    pieces = []
    for b in range(utts):
        own = labels_own_ref[pl.ds(first + b, 1), :].astype(F32)
        theirs = labels_far_ref[pl.ds(first + b, 1), :].astype(F32)
        pieces += [jnp.where(core == 0, own, theirs), jnp.where(core == 0, theirs, own)]
    label_row = jnp.concatenate(pieces, axis=1)
    for b in range(utts):
        for place, source in ((core, starts_own_ref), (1 - core, starts_far_ref)):
            starts_ref[pl.ds(b, 1), pl.ds(pl.multiple_of(place * half, half), half)] = source[
                pl.ds(first + b, 1), :
            ]
    within = iota((1, rows), 1) % positions
    token_row = jnp.where(within == 0, 0.0, pltpu.roll(label_row, 1, 1))
    label_col = column_of(label_row)
    token_col = column_of(token_row)
    vocab_lane = iota((rows, 128), 1).astype(F32)

    def one_hot(column):
        parts = [
            jnp.where(vocab_lane + float(at) == column, 1.0, 0.0).astype(BF16)
            for at in range(0, vocab, 128)
        ]
        return jnp.concatenate(parts, axis=1)

    row_within = iota((rows, width), 0) % positions
    load_table.wait()
    emb = dot(one_hot(token_col), table_ref[...])
    emb_prev = jnp.where(row_within == 0, 0.0, pltpu.roll(emb, 1, 0))
    emb_low = emb.astype(BF16)
    prev_low = emb_prev.astype(BF16)
    conv_out = dot(prev_low, taps[0]) + dot(emb_low, taps[1])
    conv_out = conv_out + conv_b_ref[...].astype(F32)[None, :]
    mean = jnp.mean(conv_out, axis=1, keepdims=True)
    centered = conv_out - mean
    rstd = lax.rsqrt(jnp.mean(centered * centered, axis=1, keepdims=True) + NORM_EPS)
    normed = centered * rstd
    gain = gain_ref[...].astype(F32)[None, :]
    scaled = normed * gain + shift_ref[...].astype(F32)[None, :]
    sigmoid = 1.0 / (1.0 + jnp.exp(-scaled))
    hidden = scaled * sigmoid
    hidden_low = hidden.astype(BF16)
    load_dec_w.wait()
    dec_proj = dot(hidden_low, dec_w_ref[...]) + dec_b_ref[...].astype(F32)[None, :]
    dec_t_ref[...] = jnp.transpose(dec_proj).astype(BF16)

    label_hot = one_hot(label_col)
    picks = pl.ds(vocab, rows)
    out_wt_ref[picks, :] = dot(label_hot, out_wt_ref[pl.ds(0, vocab), :]).astype(BF16)
    bias_ref[picks, :] = dot(label_hot, bias_ref[pl.ds(0, vocab), :].astype(BF16))
    wide_label = wide(label_col, frames // 128)
    swap_enc.wait_recv()
    project(enc_far_ref, far_lanes)

    block = 256

    def selector(b, k):
        begin = starts_ref[pl.ds(b, 1), :] + (k + b * positions)
        return iota((rows, frames), 0) == begin

    def chunk_lanes(c):
        return pl.ds(pl.multiple_of(c * frames, frames), frames)

    def utt_lanes(c):
        return pl.ds(pl.multiple_of((c // WINDOW) * frames, frames), frames)

    def activate(c):
        hot = jnp.where(selector(c // WINDOW, c % WINDOW), 1.0, 0.0).astype(BF16)
        act = jnp.tanh(enc_t_ref[:, utt_lanes(c)] + dot(dec_t_ref[...], hot))
        act_ref[c] = act
        low_ref[pl.ds(0, width), chunk_lanes(c)] = act.astype(BF16)

    def score(c, raw_ref):
        low = low_ref[pl.ds(0, width), chunk_lanes(c)]
        raw_ref[...] = dot(out_wt_ref[...], low) + wide(bias_ref[...], frames // 128)

    def normalise(c, raw_ref):
        b = c // WINDOW
        k = c % WINDOW
        top = jnp.max(raw_ref[pl.ds(0, vocab), :], axis=0, keepdims=True)
        total = jnp.zeros((1, frames), F32)
        for v in range(0, vocab, block):
            part = jnp.exp(raw_ref[pl.ds(v, block), :] - top)
            exp_ref[c, pl.ds(v, block), :] = part
            total = total + jnp.sum(part, axis=0, keepdims=True)
        log_norm = top + jnp.log(total)
        picked = selector(b, k)
        target = jnp.where(picked, raw_ref[pl.ds(vocab, rows), :], 0.0)
        target = jnp.sum(target, axis=0, keepdims=True) - log_norm
        live = starts_ref[pl.ds(b, 1), :] + k < lengths_ref[first + b]
        here = (pl.ds(k, 1), utt_lanes(c))
        blank_ref[here] = raw_ref[pl.ds(0, 1), :] - log_norm
        emit_ref[here] = jnp.where(live, target, NEGATIVE_FILL)
        inv_ref[here] = 1.0 / total
        wide_label_ref[here] = jnp.sum(jnp.where(picked, wide_label, 0.0), axis=0, keepdims=True)

    activate(0)
    activate(1)
    score(0, raw_a_ref)

    def forward(i, carry):
        c = 2 * i
        score(c + 1, raw_b_ref)
        normalise(c, raw_a_ref)
        activate(jnp.minimum(c + 2, chunks - 1))
        score(jnp.minimum(c + 2, chunks - 1), raw_a_ref)
        normalise(c + 1, raw_b_ref)
        activate(jnp.minimum(c + 3, chunks - 1))
        return carry

    lax.fori_loop(0, chunks // 2, forward, 0)

    starts_row = jnp.concatenate([starts_ref[b : b + 1, :] for b in range(utts)], axis=1)
    lane_row = iota((1, lanes), 1)
    moved = jnp.where(lane_row % frames == 0, 0, starts_row - pltpu.roll(starts_row, 1, 1))
    scale = jnp.zeros((1, lanes), F32)
    for b in range(utts):
        scale = jnp.where(lane_row // frames == b, -cot_ref[first + b] / frames, scale)
    leaving, blank_g, emit_g = lattice(blank_ref[...], emit_ref[...], moved, scale, frames)
    blank_g_ref[...] = blank_g
    emit_g_ref[...] = emit_g
    factor_ref[...] = -(blank_g + emit_g) * inv_ref[...]
    ends = iota((8, lanes), 1)
    for b in range(utts):
        last = (ends == (b + 1) * frames - 1) & (iota((8, lanes), 0) == WINDOW - 1)
        loss_ref[b] = -jnp.sum(jnp.where(last, leaving, 0.0)) / frames

    def logits_back(v):
        ids = iota((block, frames), 0) + v
        for c in range(chunks):
            b, k = c // WINDOW, c % WINDOW
            here = (slice(k, k + 1), slice(b * frames, (b + 1) * frames))
            blank_now, emit_now, factor = blank_g_ref[here], emit_g_ref[here], factor_ref[here]
            label_now = wide_label_ref[here].astype(jnp.int32)
            other_part = jnp.where(ids == 0, blank_now, 0.0) if v == 0 else 0.0
            grad = exp_ref[c, pl.ds(v, block), :] * factor + jnp.where(
                ids == label_now, emit_now, other_part
            )
            glow_ref[pl.ds(v, block), pl.ds(c * frames, frames)] = grad.astype(BF16)

    def weight_back(v):
        total = dot_nt(low_ref[...], glow_ref[pl.ds(v, block), :])
        grads_ref[v // width, :, :, :, :, pl.ds(v % width, block)] = total[:width].reshape(
            grads_ref.shape[1:5] + (block,)
        )
        small_ref[pl.ds(13 + v // width, 1), pl.ds(v % width, block)] = total[width : width + 1]

    logits_back(0)
    for v in range(0, vocab, block):
        weight_back(v)
        if v + block < vocab:
            logits_back(v + block)

    stage0(0)

    enc_sum_ref[...] = jnp.zeros(enc_sum_ref.shape, F32)
    dec_sum_ref[...] = jnp.zeros(dec_sum_ref.shape, F32)

    def pull(c, back_ref):
        back_ref[pl.ds(0, width), :] = dot(out_w_ref[...], glow_ref[:, chunk_lanes(c)])

    def settle(c, back_ref):
        act = act_ref[c]
        grad = back_ref[pl.ds(0, width), :] * (1.0 - act * act)
        enc_sum_ref[:, utt_lanes(c)] += grad
        hot = jnp.where(selector(c // WINDOW, c % WINDOW), 1.0, 0.0).astype(BF16)
        both = dot_nt(jnp.concatenate(halves(grad), axis=0), hot)
        dec_sum_ref[...] += both[:width] + both[width:]

    def backward(i, carry):
        c = 2 * i
        pull(c + 1, raw_b_ref)
        settle(c, raw_a_ref)
        pull(jnp.minimum(c + 2, chunks - 1), raw_a_ref)
        settle(c + 1, raw_b_ref)
        return carry

    pull(0, raw_a_ref)
    lax.fori_loop(0, chunks // 2, backward, 0)
    stage1(0)

    enc_b_grad = jnp.zeros((1, width), F32)
    enc_w_grad = jnp.zeros((enc_w_ref.shape[0], width), F32)
    for source, place, target in (
        (enc_far_ref, far_lanes, enc_g_send_ref),
        (enc_own_ref, own_lanes, enc_g_own_ref),
    ):
        enc_g = jnp.concatenate([enc_sum_ref[:, place(b)] for b in range(utts)], axis=1)
        enc_g = jnp.transpose(enc_g).astype(BF16)
        target[...] = enc_g.reshape(utts, half, width)
        value = source[...].reshape(utts * half, enc_w_ref.shape[0])
        enc_w_grad = enc_w_grad + dot(jnp.transpose(value), enc_g)
        enc_b_grad = enc_b_grad + jnp.sum(enc_g.astype(F32), axis=0, keepdims=True)
    grads_ref[2] = enc_w_grad.reshape(grads_ref.shape[1:])
    enc_copy = send(enc_g_send_ref, enc_g_far_hbm, enc_sems, other)
    leave(enc_g_own_ref, enc_g_own_hbm, UNITS)

    dec_g = jnp.transpose(dec_sum_ref[...]).astype(BF16)
    dec_b_grad = jnp.sum(dec_g.astype(F32), axis=0, keepdims=True)
    grads_ref[3] = dot(jnp.transpose(hidden).astype(BF16), dec_g).reshape(grads_ref.shape[1:])
    stage0(1)
    hidden_grad = dot_nt(dec_g, dec_w_ref[...])
    scaled_grad = hidden_grad * (sigmoid * (1.0 + scaled * (1.0 - sigmoid)))
    gain_grad = jnp.sum(scaled_grad * normed, axis=0, keepdims=True)
    shift_grad = jnp.sum(scaled_grad, axis=0, keepdims=True)
    normed_grad = scaled_grad * gain
    conv_grad = rstd * (
        normed_grad
        - jnp.mean(normed_grad, axis=1, keepdims=True)
        - normed * jnp.mean(normed_grad * normed, axis=1, keepdims=True)
    )
    high, rest = halves(conv_grad)
    prev_grad = dot_nt(high, taps[0]) + dot_nt(rest, taps[0])
    emb_grad = dot_nt(high, taps[1]) + dot_nt(rest, taps[1])
    emb_grad = emb_grad + jnp.where(
        row_within == positions - 1, 0.0, pltpu.roll(prev_grad, rows - 1, 0)
    )
    high, rest = halves(emb_grad)
    token_hot_t = jnp.where(
        iota((vocab, rows), 0) == token_row.astype(jnp.int32), 1.0, 0.0
    ).astype(BF16)
    for part in range(vocab // width):
        hot = token_hot_t[part * width : (part + 1) * width]
        table_grad = dot(hot, high) + dot(hot, rest)
        grads_ref[4 + part] = table_grad.reshape(grads_ref.shape[1:])
    stage0(2)

    conv_b_grad = jnp.sum(conv_grad, axis=0, keepdims=True)
    turned = halves(jnp.transpose(conv_grad))
    fold = jnp.where(iota((8, width), 1) % 4 == iota((8, width), 0), 1.0, 0.0).astype(BF16)
    for tap, source in enumerate((prev_low, emb_low)):
        outer = jnp.where(same_group, dot(turned[0], source) + dot(turned[1], source), 0.0)
        high, rest = halves(outer)
        folded = dot(fold, high) + dot(fold, rest)
        small_ref[pl.ds(4 * tap, 4), :] = folded[:4]
    for at, value in enumerate((conv_b_grad, gain_grad, shift_grad, dec_b_grad, enc_b_grad)):
        small_ref[pl.ds(8 + at, 1), :] = value

    small_step(0)
    order = (
        ((2, 0), (1, 1), (3, 0), (1, 2)),
        ((2, 1), (4, 0), (2, 2), (3, 1)),
        ((3, 2), (5, 0), (4, 1)),
        ((6, 0), (4, 2), (5, 1)),
        ((7, 0), (5, 2), (6, 1)),
        ((6, 2), (7, 1), (7, 2), (8, 1), (8, 0), (8, 2)),
    )
    stages = (stage0, stage1, stage2, stage3, stage4, stage5, stage6, stage7, stage8)
    for at, steps in enumerate(order):
        for stage, u in steps:
            stages[stage](u)
        if at in (0, 1):
            small_step(at + 1)
        elif at in (3, 4):
            small_step(at)
    small_step(5)
    for u in range(UNITS):
        all_sent(u)
    enc_copy.wait_recv()
    for copy in pending:
        copy.wait_send()
    for copy in outs:
        copy.wait()


def finish_kernel(
    share,
    loss_in_ref,
    small_hbm,
    total_hbm,
    enc_g_own_hbm,
    enc_g_far_hbm,
    enc_w_hbm,
    loss_ref,
    enc_grad_hbm,
    table_hbm,
    conv_w_hbm,
    conv_b_hbm,
    gain_hbm,
    shift_hbm,
    dec_w_hbm,
    dec_b_hbm,
    enc_w_grad_hbm,
    enc_b_hbm,
    out_w_hbm,
    out_b_hbm,
    enc_grad_ref,
    table_ref,
    dec_w_ref,
    enc_w_grad_ref,
    out_w_ref,
    total_ref,
    enc_g_own_ref,
    enc_g_far_ref,
    enc_w_ref,
    small_ref,
    conv_w_ref,
    vector_ref,
    out_b_ref,
    load_sems,
    sems,
):
    core = lax.axis_index("au")
    width = enc_w_ref.shape[1]
    loads = []
    for i in range(BLOCKS):
        loads.append((total_hbm.at[i], total_ref.at[i]))
    loads += [
        (enc_w_hbm, enc_w_ref),
        (enc_g_own_hbm, enc_g_own_ref),
        (enc_g_far_hbm, enc_g_far_ref),
        (small_hbm, small_ref),
    ]
    loads = [
        pltpu.make_async_copy(source, target, load_sems.at[at])
        for at, (source, target) in enumerate(loads)
    ]
    for load in loads:
        load.start()
    copies = []

    def leave(source, target):
        copies.append(pltpu.make_async_copy(source, target, sems.at[len(copies)]))
        copies[-1].start()

    for b in range(share):
        loss_ref[b] = loss_in_ref[b]
    every = pl.ds(0, width)
    for i, target, home, where in (
        (0, out_w_ref, out_w_hbm, (every, pl.ds(0, width))),
        (1, out_w_ref, out_w_hbm, (every, pl.ds(width, width))),
        (2, enc_w_grad_ref, enc_w_grad_hbm, (every, every)),
        (3, dec_w_ref, dec_w_hbm, (every, every)),
        (4, table_ref, table_hbm, (pl.ds(0, width), every)),
        (5, table_ref, table_hbm, (pl.ds(width, width), every)),
    ):
        loads[i].wait()
        target[where] = total_ref[i].astype(F32).reshape(width, width)
        leave(target.at[where], home.at[where])
    loads[BLOCKS].wait()
    for at, source, place in (
        (BLOCKS + 1, enc_g_own_ref, core),
        (BLOCKS + 2, enc_g_far_ref, 1 - core),
    ):
        loads[at].wait()
        utts, half, _ = source.shape
        grad = dot_nt(source[...].reshape(utts * half, width), enc_w_ref[...])
        mine = pl.ds(place * share, share)
        enc_grad_ref[mine] = grad.reshape(utts, half, enc_w_ref.shape[0])
        leave(enc_grad_ref.at[mine], enc_grad_hbm.at[mine])
    loads[BLOCKS + 3].wait()
    for at, home in enumerate((conv_b_hbm, gain_hbm, shift_hbm, dec_b_hbm, enc_b_hbm)):
        vector_ref[at, :] = small_ref[8 + at, :]
    out_b_ref[pl.ds(0, width)] = small_ref[13, :]
    out_b_ref[pl.ds(width, width)] = small_ref[14, :]
    for at, home in enumerate((conv_b_hbm, gain_hbm, shift_hbm, dec_b_hbm, enc_b_hbm)):
        leave(vector_ref.at[at], home)
    leave(out_b_ref, out_b_hbm)
    group = width // 4
    high, rest = halves(small_ref[:8, :])
    last = (small_ref[:8, :] - high.astype(F32) - rest.astype(F32)).astype(BF16)
    for i in range(4):
        take = iota((width, group), 0) == 4 * iota((width, group), 1) + i
        take = jnp.where(take, 1.0, 0.0).astype(BF16)
        picked = dot(high, take) + dot(rest, take) + dot(last, take)
        for tap in range(2):
            conv_w_ref[tap, i] = picked[4 * tap : 4 * tap + 4]
    leave(conv_w_ref, conv_w_hbm)
    for copy in copies:
        copy.wait()


def on_device(
    item_count,
    encoder_out,
    labels,
    lengths,
    starts,
    loss_cot,
    embed_table,
    conv_weight,
    conv_bias,
    norm_gain,
    norm_bias,
    dec_weight,
    dec_bias,
    enc_weight,
    enc_bias,
    out_weight,
    out_bias,
):
    utt_count, half, enc_dim = encoder_out.shape
    dec_dim = embed_table.shape[1]
    width, vocab = out_weight.shape
    share = utt_count // 2
    frames = 2 * half
    pairs = share * frames * WINDOW
    rows = share * 2 * labels.shape[1]
    lanes = share * frames
    chunks = share * WINDOW
    rounds = (item_count // 16).bit_length() - 1
    split = (2, 2, 2, width // 8, width)
    deep = max(rounds, 1)
    vmem = pl.BlockSpec(memory_space=pltpu.VMEM)
    smem = pl.BlockSpec(memory_space=pltpu.SMEM)
    anywhere = pl.BlockSpec(memory_space=pl.ANY)
    struct = jax.ShapeDtypeStruct
    mem = pltpu.VMEM
    dma = pltpu.SemaphoreType.DMA
    code = jnp.int16

    losses, enc_g_own, enc_g_far, small, totals = pl.pallas_call(
        functools.partial(main_kernel, share, rounds),
        out_shape=(
            struct((share,), F32),
            struct((share, half, width), BF16),
            struct((share, half, width), BF16),
            struct((16, width), F32),
            struct((BLOCKS,) + split, BF16),
        ),
        in_specs=[smem] * 2 + [vmem] * 9 + [anywhere] * 5,
        out_specs=(smem,) + (anywhere,) * 4,
        scratch_shapes=[
            mem(labels.shape, labels.dtype),
            mem(starts.shape, starts.dtype),
            mem((share, half, enc_dim), BF16),
            mem((share, half, enc_dim), BF16),
            mem(embed_table.shape, BF16),
            mem(dec_weight.shape, BF16),
            mem(enc_weight.shape, BF16),
            mem(out_weight.shape, BF16),
            mem((vocab + rows, width), BF16),
            mem((vocab + rows, 128), F32),
            mem((width, rows), BF16),
            mem((width, lanes), F32),
            mem((vocab + rows, frames), F32),
            mem((vocab + rows, frames), F32),
            mem((chunks, vocab, frames), F32),
            mem((chunks, width, frames), F32),
            mem((width + 16, pairs), BF16),
            mem((vocab, pairs), BF16),
        ]
        + [mem((8, lanes), F32)] * 7
        + [
            mem((width, lanes), F32),
            mem((width, rows), F32),
            mem((8, frames), jnp.int32),
            mem((BLOCKS,) + split, F32),
            mem((16, width), F32),
            mem((share, half, width), BF16),
            mem((share, half, width), BF16),
            mem((BLOCKS,) + split, BF16),
            mem((16, width), F32),
        ]
        + [
            mem((UNITS, 2) + split[1:], code),
            mem((UNITS, 2) + split[2:], code),
            mem((UNITS, 2) + split[3:], code),
        ]
        * 2
        + [
            mem((UNITS, 2, split[3], width), code),
            mem((UNITS, 3, 2, split[3] // 4, width), code),
            mem((UNITS, 6, 2, 1, width), F32),
            mem((UNITS, 6, 2, 1, width), F32),
            mem((3 + rounds, 8, width), F32),
            mem((6 + rounds, 8, width), F32),
            mem((deep, BLOCKS, split[3] // 4, width), F32),
            mem((deep, BLOCKS, split[3] // 4, width), F32),
            dma((5,)),
            dma((3, 2)),
            dma((UNITS, 6)),
            dma((UNITS, 6)),
            dma((UNITS, 6)),
            dma((UNITS, 3)),
            dma((7 + rounds, 2)),
            dma((deep, BLOCKS, 2)),
            dma((2,)),
            dma((UNITS + 2,)),
        ],
        compiler_params=pltpu.CompilerParams(
            collective_id=0, has_side_effects=True, vmem_limit_bytes=58 * MIB
        ),
        name="main",
    )(
        lengths,
        loss_cot,
        labels,
        starts,
        jnp.transpose(conv_weight, (0, 2, 3, 1)),
        conv_bias,
        norm_gain,
        norm_bias,
        dec_bias,
        enc_bias,
        out_bias,
        encoder_out,
        embed_table,
        dec_weight,
        enc_weight,
        out_weight,
    )

    vector = struct((width,), F32)
    square = struct((width, width), F32)
    outs = pl.pallas_call(
        functools.partial(finish_kernel, share),
        out_shape=(
            struct((share,), F32),
            struct(encoder_out.shape, F32),
            struct(embed_table.shape, F32),
            struct((2, 4, 4, dec_dim // 4), F32),
            vector,
            vector,
            vector,
            square,
            vector,
            square,
            vector,
            struct(out_weight.shape, F32),
            struct(out_bias.shape, F32),
        ),
        in_specs=[smem] + [anywhere] * 5,
        out_specs=(smem,) + (anywhere,) * 12,
        scratch_shapes=[
            mem(encoder_out.shape, F32),
            mem(embed_table.shape, F32),
            mem((width, width), F32),
            mem((width, width), F32),
            mem(out_weight.shape, F32),
            mem((BLOCKS,) + split, BF16),
            mem((share, half, width), BF16),
            mem((share, half, width), BF16),
            mem(enc_weight.shape, BF16),
            mem((16, width), F32),
            mem((2, 4, 4, dec_dim // 4), F32),
            mem((8, width), F32),
            mem(out_bias.shape, F32),
            dma((BLOCKS + 4,)),
            dma((BLOCKS + 9,)),
        ],
        compiler_params=pltpu.CompilerParams(vmem_limit_bytes=62 * MIB),
        name="finish",
    )(losses, small, totals, enc_g_own, enc_g_far, enc_weight)
    return outs[:3] + (jnp.transpose(outs[3], (0, 3, 1, 2)),) + outs[4:]


def solution(mesh):
    in_specs = (
        P("items", "au", None),
        P("items", "au"),
        P("items"),
        P("items", "au"),
        P("items"),
    ) + (P(),) * 11
    out_specs = (P(("items", "au")), P("items", "au", None)) + (P(),) * 11
    return jax.shard_map(
        functools.partial(on_device, mesh.shape["items"]),
        mesh=mesh,
        in_specs=in_specs,
        out_specs=out_specs,
        check_vma=False,
    )
```
